32 devices in a mesh: space: 8 (over z, y), shot: 4 (over x, core).
Axes of the slice: x: 2, y: 2, z: 4, core: 2. Of those that a mesh axis runs over, the one named last changes fastest.
Arguments:
- velocity: float32 [64, 192, 128], P('space'), may hold values from 1.5 to 4.5
- wave_now: float32 [4, 64, 192, 128], P('shot', 'space'), may hold values from -6 to 6
- wave_prev: float32 [4, 64, 192, 128], P('shot', 'space'), may hold values from -6 to 6
- adjoint_now: float32 [4, 64, 192, 128], P('shot', 'space'), may hold values from -6 to 6
- adjoint_prev: float32 [4, 64, 192, 128], P('shot', 'space'), may hold values from -6 to 6
- source_cells: int32 [4, 128], P('shot'), may hold values from 0 to 1572863, as said below
- wavelet: float32 [4, 10, 128], P('shot'), may hold values from -24 to 24
- receiver_cells: int32 [4096], P('space'), may hold values from 0 to 196607, as said below
- receiver_counts: int32 [8], P('space'), may hold values from 128 to 512, as said below
- observed: float32 [4, 10, 4096], P('shot', None, 'space'), may hold values from -24 to 24
Outputs:
- gradient: float32 [64, 192, 128], P('space', 'shot')
The draws below stay inside these ranges and needn't reach their ends.
Inputs may be any that keep to these rules, and one draw needn't show every extreme that they name: `source_cells`: flat indices into the whole grid (first dimension slowest); the 128 cells of one shot group are distinct. `receiver_cells`: flat indices within one device's block of 8 x 192 x 128 cells (first dimension slowest); the 512 cells of one block are distinct. `receiver_counts`: the live slots of a block come first.
All inputs are finite; a program needn't handle non-finite values.
Results may differ from the reference program's by a relative error of at most 0.00002.
Values sent between devices are 32-bit elements; how exact they have to be, the bound alone decides.
A program may use at most 64 MiB of HBM per device.

```python
import jax
import jax.numpy as jnp
from jax import lax

CX = 8
NY = 192
NZ = 128
STEPS = 10
NSRC = 128
RB = 512
SHOTS = 4
SLABS = 8
NX = 64
RECS = 4096


def draw_source_cells(key, part):
    stride = NX * NY * NZ // NSRC
    baseline = jnp.arange(NSRC, dtype=jnp.int32) * stride
    jitter = jax.random.randint(jax.random.fold_in(key, 11), (SHOTS, NSRC), 0, stride, dtype=jnp.int32)
    return baseline[None, :] + jitter


def draw_receiver_cells(key, part):
    stride = CX * NY * NZ // RB
    slot_ids = jnp.arange(RECS, dtype=jnp.int32) % RB
    jitter = jax.random.randint(jax.random.fold_in(key, 12), (RECS,), 0, stride, dtype=jnp.int32)
    return slot_ids * stride + jitter


def draw_receiver_counts(key, part):
    baseline = jax.random.randint(jax.random.fold_in(key, 13), (SLABS,), RB // 4, RB + 1, dtype=jnp.int32)
    fullest = jax.random.randint(jax.random.fold_in(key, 14), (), 0, SLABS, dtype=jnp.int32)
    lowest = (fullest + 1 + jax.random.randint(jax.random.fold_in(key, 15), (), 0, SLABS - 1, dtype=jnp.int32)) % SLABS
    slab_ids = jnp.arange(SLABS, dtype=jnp.int32)
    return jnp.where(slab_ids == fullest, RB, jnp.where(slab_ids == lowest, RB // 4, baseline)).astype(jnp.int32)


def shard_levels(stream_key, extent, split, smallest, largest):
    def one(axis_at, parts):
        heights = jax.random.uniform(jax.random.fold_in(jax.random.fold_in(stream_key, 6), axis_at), (parts,), jnp.float32, smallest / len(split), largest / len(split))
        return jnp.repeat(jnp.exp(heights), extent[axis_at] // parts).reshape((-1,) + (1,) * (len(extent) - axis_at - 1))

    loudness = one(*split[0])
    for cut in split[1:]:
        loudness = loudness * one(*cut)
    return loudness


def normal_values(own_key, shape, width, bound, shards=(), kind=jnp.bfloat16):
    drawn = width * jax.random.normal(own_key, shape, jnp.float32)
    if shards:
        drawn = drawn * shard_levels(own_key, shape, shards, -0.22, 0.18)
    return jnp.clip(drawn, -bound, bound).astype(kind)


def setup_inputs(seed: int = 0) -> dict:
    seeds = jax.random.split(jax.random.key(seed), 11)
    velocity = jnp.clip(1.5 + 3.0 * jax.random.uniform(seeds[0], (NX, NY, NZ), jnp.float32) ** shard_levels(seeds[0], (NX, NY, NZ), ((0, 8),), -0.2, 0.2), 1.5, 4.5)
    wave_now = normal_values(seeds[1], (SHOTS, NX, NY, NZ), 1.0, 6.0, ((0, 4), (1, 8)), jnp.float32)
    wave_prev = normal_values(seeds[2], (SHOTS, NX, NY, NZ), 1.0, 6.0, ((0, 4), (1, 8)), jnp.float32)
    adjoint_now = normal_values(seeds[3], (SHOTS, NX, NY, NZ), 1.0, 6.0, ((0, 4), (1, 8)), jnp.float32)
    adjoint_prev = normal_values(seeds[4], (SHOTS, NX, NY, NZ), 1.0, 6.0, ((0, 4), (1, 8)), jnp.float32)
    source_cells = draw_source_cells(jax.random.fold_in(seeds[10], 71), 0)
    wavelet = normal_values(seeds[6], (SHOTS, STEPS, NSRC), 4.0, 24.0, ((0, 4),), jnp.float32)
    receiver_cells = draw_receiver_cells(jax.random.fold_in(seeds[10], 71), 0)
    receiver_counts = draw_receiver_counts(jax.random.fold_in(seeds[10], 71), 0)
    observed = normal_values(seeds[9], (SHOTS, STEPS, RECS), 4.0, 24.0, ((0, 4), (2, 8)), jnp.float32)
    return {"velocity": velocity, "wave_now": wave_now, "wave_prev": wave_prev, "adjoint_now": adjoint_now, "adjoint_prev": adjoint_prev, "source_cells": source_cells, "wavelet": wavelet, "receiver_cells": receiver_cells, "receiver_counts": receiver_counts, "observed": observed}


TAPS = (-205.0 / 72.0, 8.0 / 5.0, -1.0 / 5.0, 8.0 / 315.0, -1.0 / 560.0)
COURANT = 0.09


def laplace(widened):
    length_x = widened.shape[0] - 8
    extent_y = widened.shape[1]
    extent_z = widened.shape[2]
    padded = jnp.pad(widened, ((0, 0), (4, 4), (4, 4)))
    centre = widened[4:4 + length_x]
    result = (3.0 * TAPS[0]) * centre
    for distance in range(1, 5):
        beside_all = padded[4 + distance:4 + distance + length_x, 4:4 + extent_y, 4:4 + extent_z] + padded[4 - distance:4 - distance + length_x, 4:4 + extent_y, 4:4 + extent_z]
        beside_all = beside_all + padded[4:4 + length_x, 4 + distance:4 + distance + extent_y, 4:4 + extent_z] + padded[4:4 + length_x, 4 - distance:4 - distance + extent_y, 4:4 + extent_z]
        beside_all = beside_all + padded[4:4 + length_x, 4:4 + extent_y, 4 + distance:4 + distance + extent_z] + padded[4:4 + length_x, 4:4 + extent_y, 4 - distance:4 - distance + extent_z]
        result = result + TAPS[distance] * beside_all
    return result


def one_shot(courant_sq, shot_inputs, receiver_index, live_slots):
    start_now, start_prev, adjoint_start, adjoint_after, source_index, pulses, observed_shot = shot_inputs
    shape_grid = start_now.shape

    def forward(carried, source_pulse):
        current, former = carried
        widened = jnp.pad(current, ((4, 4), (0, 0), (0, 0)))
        latest = 2.0 * current - former + courant_sq * laplace(widened)
        latest = latest.reshape(-1).at[source_index].add(source_pulse).reshape(shape_grid)
        acceleration = latest - 2.0 * current + former
        return (latest, current), (acceleration, latest.reshape(-1)[receiver_index])

    _, (accelerations, traces) = lax.scan(forward, (start_now, start_prev), pulses)
    misfit = (traces - observed_shot) * live_slots

    def backward(carried, inputs):
        following, furthest, imaging = carried
        acceleration, residual = inputs
        widened = jnp.pad(following, ((4, 4), (0, 0), (0, 0)))
        earlier = 2.0 * following - furthest + courant_sq * laplace(widened)
        earlier = earlier.reshape(-1).at[receiver_index].add(residual).reshape(shape_grid)
        return (earlier, following, imaging + earlier * acceleration), None

    empty_field = jnp.zeros(shape_grid, jnp.float32)
    (_, _, imaging), _ = lax.scan(backward, (adjoint_start, adjoint_after, empty_field), (accelerations, misfit), reverse=True)
    return imaging


def reference(velocity, wave_now, wave_prev, adjoint_now, adjoint_prev, source_cells, wavelet, receiver_cells, receiver_counts, observed):
    courant_sq = (COURANT * velocity) ** 2
    slot_ids = jnp.arange(RECS, dtype=jnp.int32)
    owner_slab = slot_ids // RB
    receiver_index = (owner_slab * (CX * NY * NZ) + receiver_cells).astype(jnp.int32)
    live_slots = ((slot_ids % RB) < receiver_counts[owner_slab]).astype(jnp.float32)
    images = lax.map(lambda shot_inputs: one_shot(courant_sq, shot_inputs, receiver_index, live_slots), (wave_now, wave_prev, adjoint_now, adjoint_prev, source_cells, wavelet, observed))
    return -2.0 / velocity ** 3 * jnp.sum(images, axis=0)
```

```python
import jax
import jax.numpy as jnp
from jax import lax
from jax.experimental import pallas as pl
from jax.experimental.pallas import tpu as pltpu
from jax.sharding import PartitionSpec as P

TAPS = (-205.0 / 72.0, 8.0 / 5.0, -1.0 / 5.0, 8.0 / 315.0, -1.0 / 560.0)
COURANT = 0.09
MESH = pl.DeviceIdType.MESH
PAD = 8
H = 4
TROWS = 24
CHUNK = 32


def scatter_kernel(enc, senc, vals, svals, s_out, o_out, m_out, table):
    steps, lx, ly, lz = s_out.shape
    lines = lx * ly
    lane = lax.broadcasted_iota(jnp.int32, (8, lz), 1)

    def clear(i, _):
        table[pl.ds(pl.multiple_of(i * 64, 8), 64), :] = jnp.zeros((64, lz), jnp.float32)
        return 0

    lax.fori_loop(0, table.shape[0] // 64, clear, 0)

    def place(cells, values, first, tiles):
        loaded = [values[8 * k : 8 * k + 8, first : first + 128] for k in range(2)]

        def one(j, _):
            cell = cells[first + j]
            line = lax.shift_right_logical(cell, 7)
            z = cell & 127
            shift = (z - j) & 127
            here = lane == z
            base = pl.multiple_of(line * TROWS, 8)
            for value, tile in zip(loaded, tiles):
                at = pl.ds(pl.multiple_of(base + 8 * tile, 8), 8)
                table[at, :] = table[at, :] + jnp.where(here, pltpu.roll(value, shift, 1), 0.0)
            return 0

        lax.fori_loop(0, 128, one, 0, unroll=8)

    for first in range(0, enc.shape[0], 128):
        place(enc, vals, first, (0, 1))
    for first in range(0, senc.shape[0], 128):
        place(senc, svals, first, (2, 1))

    def spread(xi, _):
        for y0 in range(0, ly, 8):
            base = (xi * ly + y0) * TROWS
            for t in range(steps):
                o_out[t, xi, y0 : y0 + 8, :] = table[pl.ds(base + t, 8, stride=TROWS), :]
                row = 16 + t if t < 8 else 3 + t
                s_out[t, xi, y0 : y0 + 8, :] = table[pl.ds(base + row, 8, stride=TROWS), :]
            m_out[xi, y0 : y0 + 8, :] = table[pl.ds(base + 10, 8, stride=TROWS), :]
        return 0

    lax.fori_loop(0, lx, spread, 0)


def wave_kernel(
    vel, now, prev, adj, adjp, s_hbm, o_hbm, m_hbm, out,
    u, c2, velb, s_v, o_v, m_v, img, pair, red, got,
    halo_send, halo_recv, init_send, init_recv, loc, red_send, red_recv,
):
    cx, ny, nz = vel.shape
    lx, ly = 2 * cx, ny // 2
    steps = s_hbm.shape[0]
    n_space = lax.axis_size("space")
    i = lax.axis_index("space")
    s = lax.axis_index("shot")
    a, b = i // 2, i % 2
    x, core = s // 2, s % 2
    has_low = a > 0
    has_high = a < n_space // 2 - 1
    other_i = i + 1 - 2 * b
    other_s = s + 1 - 2 * core
    cross_s = s + 2 - 4 * x
    top = 2 * steps + 3

    def zero_low(l, _):
        u[l, 0:H, PAD : PAD + ly, :] = jnp.zeros((H, ly, nz), jnp.float32)
        return 0

    def zero_high(l, _):
        u[l, H + lx : lx + 2 * H, PAD : PAD + ly, :] = jnp.zeros((H, ly, nz), jnp.float32)
        return 0

    def zero_left(l, _):
        u[l, H : H + lx, 0:PAD, :] = jnp.zeros((lx, PAD, nz), jnp.float32)
        return 0

    def zero_right(l, _):
        u[l, H : H + lx, PAD + ly : 2 * PAD + ly, :] = jnp.zeros((lx, PAD, nz), jnp.float32)
        return 0

    @pl.when(jnp.logical_not(has_low))
    def _():
        lax.fori_loop(0, top, zero_low, 0)

    @pl.when(jnp.logical_not(has_high))
    def _():
        lax.fori_loop(0, top, zero_high, 0)

    @pl.when(b == 0)
    def _():
        lax.fori_loop(0, top, zero_left, 0)

    @pl.when(b == 1)
    def _():
        lax.fori_loop(0, top, zero_right, 0)

    level_of = (1, None, 0, steps + 3, steps + 2)
    sources = (now, vel, prev, adj, adjp)
    mine = pl.ds(pl.multiple_of(ly * b, 8), ly)
    theirs = pl.ds(pl.multiple_of(ly * (1 - b), 8), ly)

    def landing(k, half):
        if level_of[k] is None:
            return c2.at[pl.ds(cx * half, cx)]
        return u.at[level_of[k], pl.ds(H + cx * half, cx), PAD : PAD + ly, :]

    def view(k, rows):
        if k == 1:
            return sources[k].at[:, rows, :]
        return sources[k].at[0, :, rows, :]

    def local_copy(k):
        return pltpu.make_async_copy(view(k, mine), landing(k, b), loc.at[k])

    def partner_copy(k):
        return pltpu.make_async_remote_copy(
            src_ref=view(k, theirs), dst_ref=landing(k, b),
            send_sem=init_send.at[k], recv_sem=init_recv.at[k],
            device_id=(other_i, s), device_id_type=MESH,
        )

    extra = [
        pltpu.make_async_copy(s_hbm, s_v, loc.at[5]),
        pltpu.make_async_copy(m_hbm, m_v, loc.at[6]),
        pltpu.make_async_copy(
            vel.at[:, pl.ds(pl.multiple_of(velb.shape[1] * s, 8), velb.shape[1]), :], velb, loc.at[7]
        ),
        pltpu.make_async_copy(o_hbm, o_v, loc.at[8]),
    ]

    for k in range(5):
        local_copy(k).start()
    for copy in extra:
        copy.start()

    barrier = pltpu.get_barrier_semaphore()
    for target in ((other_i, s), (i, other_s), (i, cross_s), (other_i, cross_s)):
        pl.semaphore_signal(barrier, inc=1, device_id=target, device_id_type=MESH)

    @pl.when(has_low)
    def _():
        pl.semaphore_signal(barrier, inc=1, device_id=(i - 2, s), device_id_type=MESH)

    @pl.when(has_high)
    def _():
        pl.semaphore_signal(barrier, inc=1, device_id=(i + 2, s), device_id_type=MESH)

    pl.semaphore_wait(barrier, 4 + has_low.astype(jnp.int32) + has_high.astype(jnp.int32))

    for k in range(5):
        partner_copy(k).start()

    def send_up(l):
        return pltpu.make_async_remote_copy(
            src_ref=u.at[l, lx : lx + H, PAD : PAD + ly, :],
            dst_ref=u.at[l, 0:H, PAD : PAD + ly, :],
            send_sem=halo_send.at[l, 0], recv_sem=halo_recv.at[l, 0],
            device_id=(i + 2, s), device_id_type=MESH,
        )

    def send_down(l):
        return pltpu.make_async_remote_copy(
            src_ref=u.at[l, H : 2 * H, PAD : PAD + ly, :],
            dst_ref=u.at[l, lx + H : lx + 2 * H, PAD : PAD + ly, :],
            send_sem=halo_send.at[l, 1], recv_sem=halo_recv.at[l, 1],
            device_id=(i - 2, s), device_id_type=MESH,
        )

    def send_side(l):
        return pltpu.make_async_remote_copy(
            src_ref=u.at[l, H : H + lx, pl.ds(pl.multiple_of(ly - (ly - PAD) * b, 8), PAD), :],
            dst_ref=u.at[l, H : H + lx, pl.ds(pl.multiple_of((ly + PAD) * b, 8), PAD), :],
            send_sem=halo_send.at[l, 2], recv_sem=halo_recv.at[l, 2],
            device_id=(other_i, s), device_id_type=MESH,
        )

    def start_x(l):
        @pl.when(has_high)
        def _():
            send_up(l).start()

        @pl.when(has_low)
        def _():
            send_down(l).start()

    def wait_halos(l):
        send_side(l).wait()

        @pl.when(has_low)
        def _():
            send_up(l).wait_recv()
            send_down(l).wait_send()

        @pl.when(has_high)
        def _():
            send_down(l).wait_recv()
            send_up(l).wait_send()

    def settle(k):
        local_copy(k).wait()
        partner_copy(k).wait()

    lane = lax.broadcasted_iota(jnp.int32, (CHUNK, nz), 1)

    def laplace(l, xi, r0):
        rows = lambda d: slice(PAD + r0 + d, PAD + r0 + d + CHUNK)
        centre = u[l, H + xi, rows(0), :]
        result = 3.0 * TAPS[0] * centre
        for k in range(1, H + 1):
            beside = u[l, H + xi + k, rows(0), :] + u[l, H + xi - k, rows(0), :]
            beside = beside + u[l, H + xi, rows(k), :] + u[l, H + xi, rows(-k), :]
            beside = beside + jnp.where(lane < nz - k, pltpu.roll(centre, nz - k, 1), 0.0)
            beside = beside + jnp.where(lane >= k, pltpu.roll(centre, k, 1), 0.0)
            result = result + TAPS[k] * beside
        return centre, result

    def sweep(first, last, body):
        def layer(xi, _):
            for r0 in range(0, ly, CHUNK):
                body(xi, r0)
            return 0

        lax.fori_loop(first, last, layer, 0)

    settle(0)
    start_x(1)
    send_side(1).start()

    settle(1)

    def square(xi, r0):
        value = COURANT * c2[xi, r0 : r0 + CHUNK, :]
        c2[xi, r0 : r0 + CHUNK, :] = value * value
        img[xi, r0 : r0 + CHUNK, :] = jnp.zeros((CHUNK, nz), jnp.float32)

    sweep(0, lx, square)
    settle(2)
    for copy in extra:
        copy.wait()

    def forward(t, _):
        cur = t + 1

        def cell(xi, r0):
            rows = slice(PAD + r0, PAD + r0 + CHUNK)
            inner = slice(r0, r0 + CHUNK)
            centre, lap = laplace(cur, xi, r0)
            fresh = 2.0 * centre - u[t, H + xi, rows, :] + c2[xi, inner, :] * lap
            u[t + 2, H + xi, rows, :] = fresh + s_v[t, xi, inner, :]

        wait_halos(cur)
        sweep(0, H, cell)
        sweep(lx - H, lx, cell)

        @pl.when(t < steps - 1)
        def _():
            start_x(cur + 1)

        sweep(H, lx - H, cell)

        @pl.when(t < steps - 1)
        def _():
            send_side(cur + 1).start()

        return 0

    lax.fori_loop(0, steps, forward, 0)

    settle(3)
    settle(4)
    start_x(steps + 3)
    send_side(steps + 3).start()

    def backward(k, _):
        t = steps - 1 - k
        cur = steps + 3 + k

        def cell(xi, r0):
            rows = slice(PAD + r0, PAD + r0 + CHUNK)
            inner = slice(r0, r0 + CHUNK)
            centre, lap = laplace(cur, xi, r0)
            fresh = 2.0 * centre - u[cur - 1, H + xi, rows, :] + c2[xi, inner, :] * lap
            later = u[t + 2, H + xi, rows, :]
            fresh = fresh + m_v[xi, inner, :] * (later - o_v[t, xi, inner, :])
            accel = later - 2.0 * u[t + 1, H + xi, rows, :] + u[t, H + xi, rows, :]
            img[xi, inner, :] = img[xi, inner, :] + fresh * accel

            @pl.when(k < steps - 1)
            def _():
                u[cur + 1, H + xi, rows, :] = fresh

        wait_halos(cur)
        sweep(0, H, cell)
        sweep(lx - H, lx, cell)

        @pl.when(k < steps - 1)
        def _():
            start_x(cur + 1)

        sweep(H, lx - H, cell)

        @pl.when(k < steps - 1)
        def _():
            send_side(cur + 1).start()

        return 0

    lax.fori_loop(0, steps, backward, 0)

    band = velb.shape[1]
    keep = pl.multiple_of(band * core, 8)
    give = pl.multiple_of(band * (1 - core), 8)
    swap = pltpu.make_async_remote_copy(
        src_ref=img.at[:, pl.ds(give, band), :], dst_ref=pair,
        send_sem=red_send.at[2], recv_sem=red_recv.at[2],
        device_id=(i, other_s), device_id_type=MESH,
    )
    swap.start()
    swap.wait()

    def add_pair(xi, _):
        red[xi] = img[xi, pl.ds(keep, band), :] + pair[xi]
        return 0

    lax.fori_loop(0, lx, add_pair, 0)

    def deliver(target):
        return pltpu.make_async_remote_copy(
            src_ref=red.at[pl.ds(cx * target, cx)], dst_ref=got.at[x],
            send_sem=red_send.at[target], recv_sem=red_recv.at[x],
            device_id=(2 * a + target, 2 * b + core), device_id_type=MESH,
        )

    def arrival(k):
        return pltpu.make_async_remote_copy(
            src_ref=red.at[0:cx], dst_ref=got.at[k],
            send_sem=red_send.at[k], recv_sem=red_recv.at[k],
            device_id=(other_i, s), device_id_type=MESH,
        )

    for target in range(2):
        own = jnp.logical_and(x == b, b == target)

        @pl.when(jnp.logical_not(own))
        def _():
            deliver(target).start()

        @pl.when(own)
        def _():
            got[target] = red[cx * target : cx * (target + 1)]

    for k in range(2):
        own = jnp.logical_and(x == b, x == k)

        @pl.when(jnp.logical_not(own))
        def _():
            arrival(k).wait_recv()
            deliver(k).wait_send()

    for xi in range(cx):
        v = velb[xi]
        out[xi] = (-2.0 / (v * v * v)) * (got[0, xi] + got[1, xi])


def per_device(
    velocity, wave_now, wave_prev, adjoint_now, adjoint_prev,
    source_cells, wavelet, receiver_cells, receiver_counts, observed,
):
    cx, ny, nz = velocity.shape
    lx, ly = 2 * cx, ny // 2
    lines = lx * ly
    steps = wavelet.shape[1]
    slots = receiver_cells.shape[0]
    count = lax.axis_size("space")
    i = lax.axis_index("space")
    a, b = i // 2, i % 2
    swap = [(j, j + 1 - 2 * (j % 2)) for j in range(count)]

    live = jnp.arange(slots, dtype=jnp.int32) < receiver_counts[0]
    own_cells = jnp.where(live, receiver_cells, -1)
    their_cells = lax.ppermute(own_cells, "space", swap)
    their_obs = lax.ppermute(observed[0], "space", swap)

    def code(cells, layer0):
        line = cells // nz
        xg = line // ny + layer0
        yl = line % ny - ly * b
        ok = (cells >= 0) & (xg >= 0) & (xg < lx) & (yl >= 0) & (yl < ly)
        return jnp.where(ok, (xg * ly + yl) * nz + cells % nz, lines * nz)

    enc = jnp.concatenate([code(own_cells, cx * b), code(their_cells, cx * (1 - b))])
    senc = code(source_cells[0], -lx * a)
    vals = jnp.concatenate([observed[0], their_obs], axis=1)
    ones = jnp.ones((1, 2 * slots), jnp.float32)
    vals = jnp.concatenate([vals, ones, jnp.zeros((5, 2 * slots), jnp.float32)], axis=0)
    w = wavelet[0]
    gap = jnp.zeros((3, w.shape[1]), jnp.float32)
    svals = jnp.concatenate([w[:8], gap, w[8:], gap], axis=0)

    smem = pl.BlockSpec(memory_space=pltpu.SMEM)
    vmem = pl.BlockSpec(memory_space=pltpu.VMEM)
    anyw = pl.BlockSpec(memory_space=pl.ANY)
    f32 = jnp.float32
    dense = jax.ShapeDtypeStruct((steps, lx, ly, nz), f32)
    field = jax.ShapeDtypeStruct((lx, ly, nz), f32)
    s_f, o_f, m_f = pl.pallas_call(
        scatter_kernel,
        out_shape=(dense, dense, field),
        in_specs=[smem, smem, vmem, vmem],
        out_specs=(vmem, vmem, vmem),
        scratch_shapes=[pltpu.VMEM(((lines + 8) * TROWS, nz), f32)],
        compiler_params=pltpu.CompilerParams(vmem_limit_bytes=48 * 2**20),
        name="scatter",
    )(enc, senc, vals, svals)

    levels = 2 * steps + 3
    band = ny // 4
    dma = pltpu.SemaphoreType.DMA
    return pl.pallas_call(
        wave_kernel,
        out_shape=jax.ShapeDtypeStruct((cx, band, nz), f32),
        in_specs=[anyw] * 8,
        out_specs=vmem,
        scratch_shapes=[
            pltpu.VMEM((levels, lx + 2 * H, ly + 2 * PAD, nz), f32),
            pltpu.VMEM((lx, ly, nz), f32),
            pltpu.VMEM((cx, band, nz), f32),
            pltpu.VMEM((steps, lx, ly, nz), f32),
            pltpu.VMEM((steps, lx, ly, nz), f32),
            pltpu.VMEM((lx, ly, nz), f32),
            pltpu.VMEM((lx, ly, nz), f32),
            pltpu.VMEM((lx, band, nz), f32),
            pltpu.VMEM((lx, band, nz), f32),
            pltpu.VMEM((2, cx, band, nz), f32),
            dma((levels, 3)),
            dma((levels, 3)),
            dma((5,)),
            dma((5,)),
            dma((9,)),
            dma((3,)),
            dma((3,)),
        ],
        compiler_params=pltpu.CompilerParams(
            collective_id=0, has_side_effects=True, vmem_limit_bytes=60 * 2**20
        ),
        name="waves",
    )(velocity, wave_now, wave_prev, adjoint_now, adjoint_prev, s_f, o_f, m_f)


def solution(mesh):
    in_specs = (
        P("space", None, None),
        P("shot", "space", None, None),
        P("shot", "space", None, None),
        P("shot", "space", None, None),
        P("shot", "space", None, None),
        P("shot", None),
        P("shot", None, None),
        P("space"),
        P("space"),
        P("shot", None, "space"),
    )
    out_specs = P("space", "shot", None)
    return jax.shard_map(
        per_device, mesh=mesh, in_specs=in_specs, out_specs=out_specs, check_vma=False
    )
```

```python
import functools

import jax
import jax.numpy as jnp
from jax import lax
from jax.experimental import pallas as pl
from jax.experimental.pallas import tpu as pltpu
from jax.sharding import PartitionSpec as P

TAPS = (-205.0 / 72.0, 8.0 / 5.0, -1.0 / 5.0, 8.0 / 315.0, -1.0 / 560.0)
COURANT = 0.09
MESH = pl.DeviceIdType.MESH
PAD = 8
H = 4
TROWS = 21
CHUNK = 32


def scatter_kernel(enc, senc, vals, svals, s_out, o_out, m_out, table):
    steps, lx, ly, lz = s_out.shape
    lines = lx * ly
    lane = lax.broadcasted_iota(jnp.int32, (8, lz), 1)

    def clear(i, _):
        table[pl.ds(pl.multiple_of(i * 64, 8), 64), :] = jnp.zeros((64, lz), jnp.float32)
        return 0

    lax.fori_loop(0, table.shape[0] // 64, clear, 0)

    def place(cells, values, first, tiles):
        loaded = [values[8 * k : 8 * k + 8, first : first + 128] for k in range(2)]

        def one(j, _):
            cell = cells[first + j]
            line = lax.shift_right_logical(cell, 7)
            z = cell & 127
            shift = (z - j) & 127
            here = lane == z
            base = line * TROWS
            for value, tile in zip(loaded, tiles):
                at = pl.ds(base + 8 * tile, 8)
                table[at, :] = table[at, :] + jnp.where(here, pltpu.roll(value, shift, 1), 0.0)
            return 0

        lax.fori_loop(0, 128, one, 0, unroll=8)

    for first in range(0, enc.shape[0], 128):
        place(enc, vals, first, (0, 1))
    for first in range(0, senc.shape[0], 128):
        place(senc, svals, first, (1, 2))

    def spread(xi, _):
        for y0 in range(0, ly, 8):
            base = (xi * ly + y0) * TROWS
            for t in range(steps):
                o_out[t, xi, y0 : y0 + 8, :] = table[pl.ds(base + t, 8, stride=TROWS), :]
                row = 11 + t
                s_out[t, xi, y0 : y0 + 8, :] = table[pl.ds(base + row, 8, stride=TROWS), :]
            m_out[xi, y0 : y0 + 8, :] = table[pl.ds(base + 10, 8, stride=TROWS), :]
        return 0

    lax.fori_loop(0, lx, spread, 0)


def wave_kernel(
    vel, now, prev, adj, adjp, s_hbm, o_hbm, m_hbm, out,
    u, c2, velb, s_v, o_v, m_v, img, pair, red, got,
    halo_send, halo_recv, init_send, init_recv, adj_send, adj_recv, loc, red_send, red_recv,
):
    cx, ny, nz = vel.shape
    lx, ly = 2 * cx, ny // 2
    steps = s_hbm.shape[0]
    n_space = lax.axis_size("space")
    i = lax.axis_index("space")
    s = lax.axis_index("shot")
    a, b = i // 2, i % 2
    x, core = s // 2, s % 2
    has_low = a > 0
    has_high = a < n_space // 2 - 1
    other_i = i + 1 - 2 * b
    other_s = s + 1 - 2 * core
    cross_s = s + 2 - 4 * x
    top = 2 * steps + 3

    def zero_low(l, _):
        u[l, 0:H, PAD : PAD + ly, :] = jnp.zeros((H, ly, nz), jnp.float32)
        return 0

    def zero_high(l, _):
        u[l, H + lx : lx + 2 * H, PAD : PAD + ly, :] = jnp.zeros((H, ly, nz), jnp.float32)
        return 0

    def zero_left(l, _):
        u[l, H : H + lx, 0:PAD, :] = jnp.zeros((lx, PAD, nz), jnp.float32)
        return 0

    def zero_right(l, _):
        u[l, H : H + lx, PAD + ly : 2 * PAD + ly, :] = jnp.zeros((lx, PAD, nz), jnp.float32)
        return 0

    @pl.when(jnp.logical_not(has_low))
    def _():
        lax.fori_loop(0, top, zero_low, 0)

    @pl.when(jnp.logical_not(has_high))
    def _():
        lax.fori_loop(0, top, zero_high, 0)

    @pl.when(b == 0)
    def _():
        lax.fori_loop(0, top, zero_left, 0)

    @pl.when(b == 1)
    def _():
        lax.fori_loop(0, top, zero_right, 0)

    level_of = (1, None, 0, steps + 3, steps + 2)
    sources = (now, vel, prev, adj, adjp)
    mine = pl.ds(pl.multiple_of(ly * b, 8), ly)
    theirs = pl.ds(pl.multiple_of(ly * (1 - b), 8), ly)

    def landing(k, half):
        if level_of[k] is None:
            return c2.at[pl.ds(cx * half, cx)]
        return u.at[level_of[k], pl.ds(H + cx * half, cx), PAD : PAD + ly, :]

    def view(k, rows):
        if k == 1:
            return sources[k].at[:, rows, :]
        return sources[k].at[0, :, rows, :]

    def local_copy(k):
        return pltpu.make_async_copy(view(k, mine), landing(k, b), loc.at[k])

    def partner_copy(k):
        return pltpu.make_async_remote_copy(
            src_ref=view(k, theirs), dst_ref=landing(k, b),
            send_sem=init_send.at[k], recv_sem=init_recv.at[k],
            device_id=(other_i, s), device_id_type=MESH,
        )

    def partner_layer(k, layer):
        return pltpu.make_async_remote_copy(
            src_ref=sources[k].at[0, layer, theirs, :],
            dst_ref=u.at[level_of[k], H + cx * b + layer, PAD : PAD + ly, :],
            send_sem=adj_send.at[k - 3, layer], recv_sem=adj_recv.at[k - 3, layer],
            device_id=(other_i, s), device_id_type=MESH,
        )

    extra = [
        pltpu.make_async_copy(s_hbm, s_v, loc.at[5]),
        pltpu.make_async_copy(m_hbm, m_v, loc.at[6]),
        pltpu.make_async_copy(
            vel.at[:, pl.ds(pl.multiple_of(velb.shape[1] * s, 8), velb.shape[1]), :], velb, loc.at[7]
        ),
        pltpu.make_async_copy(o_hbm, o_v, loc.at[8]),
    ]

    for k in range(5):
        local_copy(k).start()
    for copy in extra:
        copy.start()

    barrier = pltpu.get_barrier_semaphore()
    for target in ((other_i, s), (i, other_s), (i, cross_s), (other_i, cross_s)):
        pl.semaphore_signal(barrier, inc=1, device_id=target, device_id_type=MESH)

    @pl.when(has_low)
    def _():
        pl.semaphore_signal(barrier, inc=1, device_id=(i - 2, s), device_id_type=MESH)

    @pl.when(has_high)
    def _():
        pl.semaphore_signal(barrier, inc=1, device_id=(i + 2, s), device_id_type=MESH)

    pl.semaphore_wait(barrier, 4 + has_low.astype(jnp.int32) + has_high.astype(jnp.int32))

    for k in range(3):
        partner_copy(k).start()

    pieces = ly // CHUNK

    def send_up(l, p):
        rows = slice(PAD + CHUNK * p, PAD + CHUNK * (p + 1))
        return pltpu.make_async_remote_copy(
            src_ref=u.at[l, lx : lx + H, rows, :],
            dst_ref=u.at[l, 0:H, rows, :],
            send_sem=halo_send.at[l, p], recv_sem=halo_recv.at[l, p],
            device_id=(i + 2, s), device_id_type=MESH,
        )

    def send_down(l, p):
        rows = slice(PAD + CHUNK * p, PAD + CHUNK * (p + 1))
        return pltpu.make_async_remote_copy(
            src_ref=u.at[l, H : 2 * H, rows, :],
            dst_ref=u.at[l, lx + H : lx + 2 * H, rows, :],
            send_sem=halo_send.at[l, pieces + p], recv_sem=halo_recv.at[l, pieces + p],
            device_id=(i - 2, s), device_id_type=MESH,
        )

    def send_side(l):
        return pltpu.make_async_remote_copy(
            src_ref=u.at[l, H : H + lx, pl.ds(pl.multiple_of(ly - (ly - PAD) * b, 8), PAD), :],
            dst_ref=u.at[l, H : H + lx, pl.ds(pl.multiple_of((ly + PAD) * b, 8), PAD), :],
            send_sem=halo_send.at[l, 2 * pieces], recv_sem=halo_recv.at[l, 2 * pieces],
            device_id=(other_i, s), device_id_type=MESH,
        )

    def start_down(l, p):
        @pl.when(has_low)
        def _():
            send_down(l, p).start()

    def start_up(l, p):
        @pl.when(has_high)
        def _():
            send_up(l, p).start()

    def start_all(l, order):
        send_side(l).start()
        for p in order:
            start_down(l, p)
            start_up(l, p)

    def wait_low(l, p):
        @pl.when(has_low)
        def _():
            send_up(l, p).wait_recv()
            send_down(l, p).wait_send()

    def wait_high(l, p):
        @pl.when(has_high)
        def _():
            send_down(l, p).wait_recv()
            send_up(l, p).wait_send()

    def settle(k):
        local_copy(k).wait()
        partner_copy(k).wait()

    lane = lax.broadcasted_iota(jnp.int32, (CHUNK, nz), 1)

    def laplace(l, xi, r0):
        rows = lambda d: slice(PAD + r0 + d, PAD + r0 + d + CHUNK)
        centre = u[l, H + xi, rows(0), :]
        result = 3.0 * TAPS[0] * centre
        for k in range(1, H + 1):
            beside = u[l, H + xi + k, rows(0), :] + u[l, H + xi - k, rows(0), :]
            beside = beside + u[l, H + xi, rows(k), :] + u[l, H + xi, rows(-k), :]
            beside = beside + jnp.where(lane < nz - k, pltpu.roll(centre, nz - k, 1), 0.0)
            beside = beside + jnp.where(lane >= k, pltpu.roll(centre, k, 1), 0.0)
            result = result + TAPS[k] * beside
        return centre, result

    def sweep(first, last, p, body):
        def layer(xi, _):
            body(xi, CHUNK * p)
            return 0

        lax.fori_loop(first, last, layer, 0, unroll=2)

    def step(cur, more, order, cell):
        for n, p in enumerate(order):
            if n == 0:
                send_side(cur).wait()
            wait_low(cur, p)
            sweep(0, H, p, cell)

            @pl.when(more)
            def _():
                start_down(cur + 1, p)

            wait_high(cur, p)
            sweep(lx - H, lx, p, cell)

            @pl.when(more)
            def _():
                start_up(cur + 1, p)

            sweep(H, lx - H, p, cell)
            if n == 0:

                @pl.when(more)
                def _():
                    send_side(cur + 1).start()

    def square(xi, r0):
        value = COURANT * c2[xi, r0 : r0 + CHUNK, :]
        c2[xi, r0 : r0 + CHUNK, :] = value * value
        img[xi, r0 : r0 + CHUNK, :] = jnp.zeros((CHUNK, nz), jnp.float32)

    def forward(order, t, _):
        cur = t + 1

        def cell(xi, r0):
            rows = slice(PAD + r0, PAD + r0 + CHUNK)
            inner = slice(r0, r0 + CHUNK)
            centre, lap = laplace(cur, xi, r0)
            fresh = 2.0 * centre - u[t, H + xi, rows, :] + c2[xi, inner, :] * lap
            u[t + 2, H + xi, rows, :] = fresh + s_v[t, xi, inner, :]

        @pl.when(t < cx)
        def _():
            partner_layer(3, t).start()
            partner_layer(4, t).start()

        step(cur, t < steps - 1, order, cell)

        @pl.when(t == steps - 2)
        def _():
            for k in (3, 4):
                local_copy(k).wait()

                def arrive(layer, _):
                    partner_layer(k, layer).wait()
                    return 0

                lax.fori_loop(0, cx, arrive, 0)
            start_all(steps + 3, order)

        return 0

    def backward(order, k, _):
        t = steps - 1 - k
        cur = steps + 3 + k

        def cell(xi, r0):
            rows = slice(PAD + r0, PAD + r0 + CHUNK)
            inner = slice(r0, r0 + CHUNK)
            centre, lap = laplace(cur, xi, r0)
            fresh = 2.0 * centre - u[cur - 1, H + xi, rows, :] + c2[xi, inner, :] * lap
            later = u[t + 2, H + xi, rows, :]
            fresh = fresh + m_v[xi, inner, :] * (later - o_v[t, xi, inner, :])
            accel = later - 2.0 * u[t + 1, H + xi, rows, :] + u[t, H + xi, rows, :]
            img[xi, inner, :] = img[xi, inner, :] + fresh * accel
            u[cur + 1, H + xi, rows, :] = fresh

        step(cur, k < steps - 1, order, cell)
        return 0

    def both(order):
        settle(0)
        start_all(1, order)
        settle(1)
        for p in order:
            sweep(0, lx, p, square)
        settle(2)
        for copy in extra:
            copy.wait()
        lax.fori_loop(0, steps, functools.partial(forward, order), 0)
        lax.fori_loop(0, steps, functools.partial(backward, order), 0)

    @pl.when(b == 0)
    def _():
        both(tuple(range(pieces - 1, -1, -1)))

    @pl.when(b == 1)
    def _():
        both(tuple(range(pieces)))

    band = velb.shape[1]
    keep = pl.multiple_of(band * core, 8)
    give = pl.multiple_of(band * (1 - core), 8)
    swap = pltpu.make_async_remote_copy(
        src_ref=img.at[:, pl.ds(give, band), :], dst_ref=pair,
        send_sem=red_send.at[2], recv_sem=red_recv.at[2],
        device_id=(i, other_s), device_id_type=MESH,
    )
    swap.start()
    swap.wait()

    def add_pair(xi, _):
        red[xi] = img[xi, pl.ds(keep, band), :] + pair[xi]
        return 0

    lax.fori_loop(0, lx, add_pair, 0)

    def deliver(target):
        return pltpu.make_async_remote_copy(
            src_ref=red.at[pl.ds(cx * target, cx)], dst_ref=got.at[x],
            send_sem=red_send.at[target], recv_sem=red_recv.at[x],
            device_id=(2 * a + target, 2 * b + core), device_id_type=MESH,
        )

    def arrival(k):
        return pltpu.make_async_remote_copy(
            src_ref=red.at[0:cx], dst_ref=got.at[k],
            send_sem=red_send.at[k], recv_sem=red_recv.at[k],
            device_id=(other_i, s), device_id_type=MESH,
        )

    for target in range(2):
        own = jnp.logical_and(x == b, b == target)

        @pl.when(jnp.logical_not(own))
        def _():
            deliver(target).start()

        @pl.when(own)
        def _():
            got[target] = red[cx * target : cx * (target + 1)]

    for k in range(2):
        own = jnp.logical_and(x == b, x == k)

        @pl.when(jnp.logical_not(own))
        def _():
            arrival(k).wait_recv()
            deliver(k).wait_send()

    for xi in range(cx):
        v = velb[xi]
        out[xi] = (-2.0 / (v * v * v)) * (got[0, xi] + got[1, xi])


def per_device(
    velocity, wave_now, wave_prev, adjoint_now, adjoint_prev,
    source_cells, wavelet, receiver_cells, receiver_counts, observed,
):
    cx, ny, nz = velocity.shape
    lx, ly = 2 * cx, ny // 2
    lines = lx * ly
    steps = wavelet.shape[1]
    slots = receiver_cells.shape[0]
    count = lax.axis_size("space")
    i = lax.axis_index("space")
    a, b = i // 2, i % 2
    swap = [(j, j + 1 - 2 * (j % 2)) for j in range(count)]

    live = jnp.arange(slots, dtype=jnp.int32) < receiver_counts[0]
    own_cells = jnp.where(live, receiver_cells, -1)
    their_cells = lax.ppermute(own_cells, "space", swap)
    their_obs = lax.ppermute(observed[0], "space", swap)

    def code(cells, layer0):
        line = cells // nz
        xg = line // ny + layer0
        yl = line % ny - ly * b
        ok = (cells >= 0) & (xg >= 0) & (xg < lx) & (yl >= 0) & (yl < ly)
        return jnp.where(ok, (xg * ly + yl) * nz + cells % nz, lines * nz)

    enc = jnp.concatenate([code(own_cells, cx * b), code(their_cells, cx * (1 - b))])
    senc = code(source_cells[0], -lx * a)
    vals = jnp.concatenate([observed[0], their_obs], axis=1)
    ones = jnp.ones((1, 2 * slots), jnp.float32)
    vals = jnp.concatenate([vals, ones, jnp.zeros((5, 2 * slots), jnp.float32)], axis=0)
    w = wavelet[0]
    gap = jnp.zeros((3, w.shape[1]), jnp.float32)
    svals = jnp.concatenate([gap, w, gap], axis=0)

    smem = pl.BlockSpec(memory_space=pltpu.SMEM)
    vmem = pl.BlockSpec(memory_space=pltpu.VMEM)
    anyw = pl.BlockSpec(memory_space=pl.ANY)
    f32 = jnp.float32
    dense = jax.ShapeDtypeStruct((steps, lx, ly, nz), f32)
    field = jax.ShapeDtypeStruct((lx, ly, nz), f32)
    s_f, o_f, m_f = pl.pallas_call(
        scatter_kernel,
        out_shape=(dense, dense, field),
        in_specs=[smem, smem, vmem, vmem],
        out_specs=(vmem, vmem, vmem),
        scratch_shapes=[pltpu.VMEM(((lines + 64) * TROWS, nz), f32)],
        compiler_params=pltpu.CompilerParams(vmem_limit_bytes=48 * 2**20),
        name="scatter",
    )(enc, senc, vals, svals)

    levels = 2 * steps + 4
    band = ny // 4
    dma = pltpu.SemaphoreType.DMA
    return pl.pallas_call(
        wave_kernel,
        out_shape=jax.ShapeDtypeStruct((cx, band, nz), f32),
        in_specs=[anyw] * 8,
        out_specs=vmem,
        scratch_shapes=[
            pltpu.VMEM((levels, lx + 2 * H, ly + 2 * PAD, nz), f32),
            pltpu.VMEM((lx, ly, nz), f32),
            pltpu.VMEM((cx, band, nz), f32),
            pltpu.VMEM((steps, lx, ly, nz), f32),
            pltpu.VMEM((steps, lx, ly, nz), f32),
            pltpu.VMEM((lx, ly, nz), f32),
            pltpu.VMEM((lx, ly, nz), f32),
            pltpu.VMEM((lx, band, nz), f32),
            pltpu.VMEM((lx, band, nz), f32),
            pltpu.VMEM((2, cx, band, nz), f32),
            dma((levels, 2 * (ly // CHUNK) + 1)),
            dma((levels, 2 * (ly // CHUNK) + 1)),
            dma((3,)),
            dma((3,)),
            dma((2, cx)),
            dma((2, cx)),
            dma((9,)),
            dma((3,)),
            dma((3,)),
        ],
        compiler_params=pltpu.CompilerParams(
            collective_id=0, has_side_effects=True, vmem_limit_bytes=60 * 2**20
        ),
        name="waves",
    )(velocity, wave_now, wave_prev, adjoint_now, adjoint_prev, s_f, o_f, m_f)


def solution(mesh):
    in_specs = (
        P("space", None, None),
        P("shot", "space", None, None),
        P("shot", "space", None, None),
        P("shot", "space", None, None),
        P("shot", "space", None, None),
        P("shot", None),
        P("shot", None, None),
        P("space"),
        P("space"),
        P("shot", None, "space"),
    )
    out_specs = P("space", "shot", None)
    return jax.shard_map(
        per_device, mesh=mesh, in_specs=in_specs, out_specs=out_specs, check_vma=False
    )
```

```python
import functools

import jax
import jax.numpy as jnp
from jax import lax
from jax.experimental import pallas as pl
from jax.experimental.pallas import tpu as pltpu
from jax.sharding import PartitionSpec as P

TAPS = (-205.0 / 72.0, 8.0 / 5.0, -1.0 / 5.0, 8.0 / 315.0, -1.0 / 560.0)
COURANT = 0.09
MESH = pl.DeviceIdType.MESH
PAD = 8
H = 4
TROWS = 21
CHUNK = 32


def scatter_kernel(
    enc, senc, vals, svals, s_out, o_out, m_out, low, high, s_v, o_v, m_v, sems
):
    steps, lx, ly, lz = s_v.shape
    half = lx // 2
    slots = enc.shape[1]
    lane = lax.broadcasted_iota(jnp.int32, (8, lz), 1)

    def clear(i, _):
        at = pl.ds(pl.multiple_of(i * 64, 8), 64)
        low[at, :] = jnp.zeros((64, lz), jnp.float32)
        high[at, :] = jnp.zeros((64, lz), jnp.float32)
        return 0

    lax.fori_loop(0, low.shape[0] // 64, clear, 0)

    def place(cells, values, first, tiles):
        def one(j, _):
            places = []
            for h, table in enumerate((low, high)):
                cell = cells[h, first + j]
                line = lax.shift_right_logical(cell, 7)
                z = cell & 127
                shift = (z - j) & 127
                here = lane == z
                for k, tile in enumerate(tiles):
                    value = values[h % values.shape[0], 8 * k : 8 * k + 8, first : first + 128]
                    at = pl.ds(line * TROWS + 8 * tile, 8)
                    added = jnp.where(here, pltpu.roll(value, shift, 1), 0.0)
                    places.append((table, at, table[at, :] + added))
            for table, at, value in places:
                table[at, :] = value
            return 0

        lax.fori_loop(0, 128, one, 0, unroll=8)

    for first in range(0, slots, 128):
        place(enc, vals, first, (0, 1))
    for first in range(0, senc.shape[1], 128):
        place(senc, svals, first, (1, 2))

    def copies(xi):
        return (
            pltpu.make_async_copy(s_v.at[:, xi], s_out.at[:, xi], sems.at[0, xi]),
            pltpu.make_async_copy(o_v.at[:, xi], o_out.at[:, xi], sems.at[1, xi]),
            pltpu.make_async_copy(m_v.at[xi], m_out.at[xi], sems.at[2, xi]),
        )

    for h, table in enumerate((low, high)):

        def spread(x0, _):
            xi = x0 + half * h
            for y0 in range(0, ly, 8):
                base = (x0 * ly + y0) * TROWS
                for t in range(steps):
                    o_v[t, xi, y0 : y0 + 8, :] = table[pl.ds(base + t, 8, stride=TROWS), :]
                    s_v[t, xi, y0 : y0 + 8, :] = table[pl.ds(base + 11 + t, 8, stride=TROWS), :]
                m_v[xi, y0 : y0 + 8, :] = table[pl.ds(base + 10, 8, stride=TROWS), :]
            for copy in copies(xi):
                copy.start()
            return 0

        lax.fori_loop(0, half, spread, 0)

    def finish(xi, _):
        for copy in copies(xi):
            copy.wait()
        return 0

    lax.fori_loop(0, lx, finish, 0)


def wave_kernel(
    vel, now, prev, adj, adjp, far, same, cross, s_hbm, o_hbm, m_hbm, out,
    u, c2, velb, s_v, o_v, m_v, img, pair, red, got,
    halo_send, halo_recv, adj_send, adj_recv, loc, s_sem, red_send, red_recv,
):
    cx, ny, nz = vel.shape
    lx, ly = 2 * cx, ny // 2
    steps = s_hbm.shape[0]
    n_space = lax.axis_size("space")
    i = lax.axis_index("space")
    s = lax.axis_index("shot")
    a, b = i // 2, i % 2
    x, core = s // 2, s % 2
    has_low = a > 0
    has_high = a < n_space // 2 - 1
    other_i = i + 1 - 2 * b
    other_s = s + 1 - 2 * core
    cross_s = s + 2 - 4 * x
    top = 2 * steps + 3

    def zero_low(l, _):
        u[l, 0:H, PAD : PAD + ly, :] = jnp.zeros((H, ly, nz), jnp.float32)
        return 0

    def zero_high(l, _):
        u[l, H + lx : lx + 2 * H, PAD : PAD + ly, :] = jnp.zeros((H, ly, nz), jnp.float32)
        return 0

    def zero_left(l, _):
        u[l, H : H + lx, 0:PAD, :] = jnp.zeros((lx, PAD, nz), jnp.float32)
        return 0

    def zero_right(l, _):
        u[l, H : H + lx, PAD + ly : 2 * PAD + ly, :] = jnp.zeros((lx, PAD, nz), jnp.float32)
        return 0

    @pl.when(jnp.logical_not(has_low))
    def _():
        lax.fori_loop(0, top, zero_low, 0)

    @pl.when(jnp.logical_not(has_high))
    def _():
        lax.fori_loop(0, top, zero_high, 0)

    @pl.when(b == 0)
    def _():
        lax.fori_loop(0, top, zero_left, 0)

    @pl.when(b == 1)
    def _():
        lax.fori_loop(0, top, zero_right, 0)

    level_of = (1, None, 0, steps + 3, steps + 2)
    sources = (now, vel, prev, adj, adjp)
    mine = pl.ds(pl.multiple_of(ly * b, 8), ly)
    theirs = pl.ds(pl.multiple_of(ly * (1 - b), 8), ly)

    def landing(k, half):
        if level_of[k] is None:
            return c2.at[pl.ds(cx * half, cx)]
        return u.at[level_of[k], pl.ds(H + cx * half, cx), PAD : PAD + ly, :]

    def view(k, rows):
        if k == 1:
            return sources[k].at[:, rows, :]
        return sources[k].at[0, :, rows, :]

    def local_copy(k):
        return pltpu.make_async_copy(view(k, mine), landing(k, b), loc.at[k])

    def far_copy(k):
        return pltpu.make_async_copy(far.at[k], landing(k, 1 - b), loc.at[8 + k])

    def low_copy(first):
        return pltpu.make_async_copy(first, u.at[1, 0:H, PAD : PAD + ly, :], loc.at[11])

    def high_copy(first):
        return pltpu.make_async_copy(
            first, u.at[1, H + lx : lx + 2 * H, PAD : PAD + ly, :], loc.at[12]
        )

    def s_copy(k):
        return pltpu.make_async_copy(s_hbm.at[k], s_v.at[k], s_sem.at[k])

    def partner_layer(k, layer):
        return pltpu.make_async_remote_copy(
            src_ref=sources[k].at[0, layer, theirs, :],
            dst_ref=u.at[level_of[k], H + cx * b + layer, PAD : PAD + ly, :],
            send_sem=adj_send.at[k - 3, layer], recv_sem=adj_recv.at[k - 3, layer],
            device_id=(other_i, s), device_id_type=MESH,
        )

    extra = [
        pltpu.make_async_copy(m_hbm, m_v, loc.at[5]),
        pltpu.make_async_copy(
            vel.at[:, pl.ds(pl.multiple_of(velb.shape[1] * s, 8), velb.shape[1]), :], velb, loc.at[6]
        ),
        pltpu.make_async_copy(o_hbm, o_v, loc.at[7]),
    ]

    def each_edge(call):
        for parity, low, high in ((0, cross, same), (1, same, cross)):

            @pl.when(jnp.logical_and(b == parity, has_low))
            def _():
                call(low_copy(low))

            @pl.when(jnp.logical_and(b == parity, has_high))
            def _():
                call(high_copy(high))

    for k in range(3):
        local_copy(k).start()
        far_copy(k).start()
    each_edge(lambda copy: copy.start())
    for k in range(steps):
        s_copy(k).start()
    for k in (3, 4):
        local_copy(k).start()
    for copy in extra:
        copy.start()

    barrier = pltpu.get_barrier_semaphore()
    for target in ((other_i, s), (i, other_s), (i, cross_s), (other_i, cross_s)):
        pl.semaphore_signal(barrier, inc=1, device_id=target, device_id_type=MESH)

    @pl.when(has_low)
    def _():
        pl.semaphore_signal(barrier, inc=1, device_id=(i - 2, s), device_id_type=MESH)

    @pl.when(has_high)
    def _():
        pl.semaphore_signal(barrier, inc=1, device_id=(i + 2, s), device_id_type=MESH)

    pl.semaphore_wait(barrier, 4 + has_low.astype(jnp.int32) + has_high.astype(jnp.int32))


    pieces = ly // CHUNK

    def send_up(l, p):
        rows = slice(PAD + CHUNK * p, PAD + CHUNK * (p + 1))
        return pltpu.make_async_remote_copy(
            src_ref=u.at[l, lx : lx + H, rows, :],
            dst_ref=u.at[l, 0:H, rows, :],
            send_sem=halo_send.at[l, p], recv_sem=halo_recv.at[l, p],
            device_id=(i + 2, s), device_id_type=MESH,
        )

    def send_down(l, p):
        rows = slice(PAD + CHUNK * p, PAD + CHUNK * (p + 1))
        return pltpu.make_async_remote_copy(
            src_ref=u.at[l, H : 2 * H, rows, :],
            dst_ref=u.at[l, lx + H : lx + 2 * H, rows, :],
            send_sem=halo_send.at[l, pieces + p], recv_sem=halo_recv.at[l, pieces + p],
            device_id=(i - 2, s), device_id_type=MESH,
        )

    def send_side(l):
        return pltpu.make_async_remote_copy(
            src_ref=u.at[l, H : H + lx, pl.ds(pl.multiple_of(ly - (ly - PAD) * b, 8), PAD), :],
            dst_ref=u.at[l, H : H + lx, pl.ds(pl.multiple_of((ly + PAD) * b, 8), PAD), :],
            send_sem=halo_send.at[l, 2 * pieces], recv_sem=halo_recv.at[l, 2 * pieces],
            device_id=(other_i, s), device_id_type=MESH,
        )

    def start_down(l, p):
        @pl.when(has_low)
        def _():
            send_down(l, p).start()

    def start_up(l, p):
        @pl.when(has_high)
        def _():
            send_up(l, p).start()

    def start_all(l, order):
        send_side(l).start()
        for p in order:
            start_down(l, p)
            start_up(l, p)

    def wait_low(l, p, arrives):
        @pl.when(jnp.logical_and(has_low, arrives))
        def _():
            send_up(l, p).wait_recv()
            send_down(l, p).wait_send()

    def wait_high(l, p, arrives):
        @pl.when(jnp.logical_and(has_high, arrives))
        def _():
            send_down(l, p).wait_recv()
            send_up(l, p).wait_send()

    def settle(k):
        local_copy(k).wait()
        far_copy(k).wait()

    lane = lax.broadcasted_iota(jnp.int32, (CHUNK, nz), 1)

    def laplace(l, xi, r0):
        rows = lambda d: slice(PAD + r0 + d, PAD + r0 + d + CHUNK)
        centre = u[l, H + xi, rows(0), :]
        result = 3.0 * TAPS[0] * centre
        for k in range(1, H + 1):
            beside = u[l, H + xi + k, rows(0), :] + u[l, H + xi - k, rows(0), :]
            beside = beside + u[l, H + xi, rows(k), :] + u[l, H + xi, rows(-k), :]
            beside = beside + jnp.where(lane < nz - k, pltpu.roll(centre, nz - k, 1), 0.0)
            beside = beside + jnp.where(lane >= k, pltpu.roll(centre, k, 1), 0.0)
            result = result + TAPS[k] * beside
        return centre, result

    def sweep(first, last, p, body):
        def layer(xi, _):
            body(xi, CHUNK * p)
            return 0

        lax.fori_loop(first, last, layer, 0, unroll=2)

    def step(cur, arrives, more, order, cell):
        for n, p in enumerate(order):
            if n == 0:
                send_side(cur).wait()
            wait_low(cur, p, arrives)
            sweep(0, H, p, cell)

            @pl.when(more)
            def _():
                start_down(cur + 1, p)

            wait_high(cur, p, arrives)
            sweep(lx - H, lx, p, cell)

            @pl.when(more)
            def _():
                start_up(cur + 1, p)

            sweep(H, lx - H, p, cell)
            if n == 0:

                @pl.when(more)
                def _():
                    send_side(cur + 1).start()

    def square(xi, r0):
        value = COURANT * c2[xi, r0 : r0 + CHUNK, :]
        c2[xi, r0 : r0 + CHUNK, :] = value * value
        img[xi, r0 : r0 + CHUNK, :] = jnp.zeros((CHUNK, nz), jnp.float32)

    def forward(order, t, _):
        cur = t + 1

        def cell(xi, r0):
            rows = slice(PAD + r0, PAD + r0 + CHUNK)
            inner = slice(r0, r0 + CHUNK)
            centre, lap = laplace(cur, xi, r0)
            fresh = 2.0 * centre - u[t, H + xi, rows, :] + c2[xi, inner, :] * lap
            u[t + 2, H + xi, rows, :] = fresh + s_v[t, xi, inner, :]

        @pl.when(t < cx)
        def _():
            partner_layer(3, t).start()
            partner_layer(4, t).start()

        s_copy(t).wait()
        step(cur, t > 0, t < steps - 1, order, cell)

        @pl.when(t == steps - 2)
        def _():
            for k in (3, 4):
                local_copy(k).wait()

                def arrive(layer, _):
                    partner_layer(k, layer).wait()
                    return 0

                lax.fori_loop(0, cx, arrive, 0)
            start_all(steps + 3, order)

        return 0

    def backward(order, k, _):
        t = steps - 1 - k
        cur = steps + 3 + k

        def cell(xi, r0):
            rows = slice(PAD + r0, PAD + r0 + CHUNK)
            inner = slice(r0, r0 + CHUNK)
            centre, lap = laplace(cur, xi, r0)
            fresh = 2.0 * centre - u[cur - 1, H + xi, rows, :] + c2[xi, inner, :] * lap
            later = u[t + 2, H + xi, rows, :]
            fresh = fresh + m_v[xi, inner, :] * (later - o_v[t, xi, inner, :])
            accel = later - 2.0 * u[t + 1, H + xi, rows, :] + u[t, H + xi, rows, :]
            img[xi, inner, :] = img[xi, inner, :] + fresh * accel
            u[cur + 1, H + xi, rows, :] = fresh

        step(cur, True, k < steps - 1, order, cell)
        return 0

    def both(order):
        settle(0)
        send_side(1).start()
        settle(1)
        for p in order:
            sweep(0, lx, p, square)
        settle(2)
        each_edge(lambda copy: copy.wait())
        lax.fori_loop(0, steps, functools.partial(forward, order), 0)
        for copy in extra:
            copy.wait()
        lax.fori_loop(0, steps, functools.partial(backward, order), 0)

    @pl.when(b == 0)
    def _():
        both(tuple(range(pieces - 1, -1, -1)))

    @pl.when(b == 1)
    def _():
        both(tuple(range(pieces)))

    band = velb.shape[1]
    keep = pl.multiple_of(band * core, 8)
    give = pl.multiple_of(band * (1 - core), 8)
    swap = pltpu.make_async_remote_copy(
        src_ref=img.at[:, pl.ds(give, band), :], dst_ref=pair,
        send_sem=red_send.at[2], recv_sem=red_recv.at[2],
        device_id=(i, other_s), device_id_type=MESH,
    )
    swap.start()
    swap.wait()

    def add_pair(xi, _):
        red[xi] = img[xi, pl.ds(keep, band), :] + pair[xi]
        return 0

    lax.fori_loop(0, lx, add_pair, 0)

    def deliver(target):
        return pltpu.make_async_remote_copy(
            src_ref=red.at[pl.ds(cx * target, cx)], dst_ref=got.at[x],
            send_sem=red_send.at[target], recv_sem=red_recv.at[x],
            device_id=(2 * a + target, 2 * b + core), device_id_type=MESH,
        )

    def arrival(k):
        return pltpu.make_async_remote_copy(
            src_ref=red.at[0:cx], dst_ref=got.at[k],
            send_sem=red_send.at[k], recv_sem=red_recv.at[k],
            device_id=(other_i, s), device_id_type=MESH,
        )

    for target in range(2):
        own = jnp.logical_and(x == b, b == target)

        @pl.when(jnp.logical_not(own))
        def _():
            deliver(target).start()

        @pl.when(own)
        def _():
            got[target] = red[cx * target : cx * (target + 1)]

    for k in range(2):
        own = jnp.logical_and(x == b, x == k)

        @pl.when(jnp.logical_not(own))
        def _():
            arrival(k).wait_recv()
            deliver(k).wait_send()

    for xi in range(cx):
        v = velb[xi]
        out[xi] = (-2.0 / (v * v * v)) * (got[0, xi] + got[1, xi])


def per_device(
    velocity, wave_now, wave_prev, adjoint_now, adjoint_prev,
    source_cells, wavelet, receiver_cells, receiver_counts, observed,
):
    cx, ny, nz = velocity.shape
    lx, ly = 2 * cx, ny // 2
    lines = lx * ly
    steps = wavelet.shape[1]
    slots = receiver_cells.shape[0]
    count = lax.axis_size("space")
    i = lax.axis_index("space")
    a, b = i // 2, i % 2
    swap = [(j, j + 1 - 2 * (j % 2)) for j in range(count)]

    live = jnp.arange(slots, dtype=jnp.int32) < receiver_counts[0]
    own_cells = jnp.where(live, receiver_cells, -1)
    their_cells = lax.ppermute(own_cells, "space", swap)
    their_obs = lax.ppermute(observed[0], "space", swap)

    def rows_of(block, part):
        return lax.dynamic_slice_in_dim(block, ly * part, ly, 1)

    far = jnp.stack([rows_of(f, 1 - b) for f in (wave_now[0], velocity, wave_prev[0])])
    far = lax.ppermute(far, "space", swap)
    edge = lax.dynamic_slice_in_dim(wave_now[0], (cx - H) * b, H, 0)
    beyond = [(j, j + 4 * (j % 2) - 2) for j in range(count)]
    across = [(j, j + 2 * (j % 2) - 1) for j in range(count)]
    within = lambda pairs: [(j, k) for j, k in pairs if 0 <= k < count]
    same = lax.ppermute(rows_of(edge, b), "space", within(beyond))
    cross = lax.ppermute(rows_of(edge, 1 - b), "space", within(across))

    def code(cells, layer0, layers):
        line = cells // nz
        xg = line // ny + layer0
        yl = line % ny - ly * b
        ok = (cells >= 0) & (xg >= 0) & (xg < layers) & (yl >= 0) & (yl < ly)
        return jnp.where(ok, (xg * ly + yl) * nz + cells % nz, lines // 2 * nz)

    first = b == 0
    enc = code(
        jnp.stack([jnp.where(first, own_cells, their_cells), jnp.where(first, their_cells, own_cells)]),
        0, cx,
    )
    senc = jnp.stack([code(source_cells[0], -lx * a - cx * h, cx) for h in range(2)])
    vals = jnp.stack(
        [jnp.where(first, observed[0], their_obs), jnp.where(first, their_obs, observed[0])]
    )
    ones = jnp.ones((2, 1, slots), jnp.float32)
    vals = jnp.concatenate([vals, ones, jnp.zeros((2, 5, slots), jnp.float32)], axis=1)
    w = wavelet[0]
    gap = jnp.zeros((3, w.shape[1]), jnp.float32)
    svals = jnp.concatenate([gap, w, gap], axis=0)[None]

    smem = pl.BlockSpec(memory_space=pltpu.SMEM)
    vmem = pl.BlockSpec(memory_space=pltpu.VMEM)
    anyw = pl.BlockSpec(memory_space=pl.ANY)
    f32 = jnp.float32
    dense = jax.ShapeDtypeStruct((steps, lx, ly, nz), f32)
    field = jax.ShapeDtypeStruct((lx, ly, nz), f32)
    s_f, o_f, m_f = pl.pallas_call(
        scatter_kernel,
        out_shape=(dense, dense, field),
        in_specs=[smem, smem, vmem, vmem],
        out_specs=(anyw, anyw, anyw),
        scratch_shapes=[
            pltpu.VMEM(((lines // 2 + 64) * TROWS, nz), f32),
            pltpu.VMEM(((lines // 2 + 64) * TROWS, nz), f32),
            pltpu.VMEM((steps, lx, ly, nz), f32),
            pltpu.VMEM((steps, lx, ly, nz), f32),
            pltpu.VMEM((lx, ly, nz), f32),
            pltpu.SemaphoreType.DMA((3, lx)),
        ],
        compiler_params=pltpu.CompilerParams(vmem_limit_bytes=48 * 2**20),
        cost_estimate=pl.CostEstimate(flops=10**9, bytes_accessed=80 * 10**6, transcendentals=0),
        name="scatter",
    )(enc, senc, vals, svals)

    levels = 2 * steps + 4
    band = ny // 4
    dma = pltpu.SemaphoreType.DMA
    return pl.pallas_call(
        wave_kernel,
        out_shape=jax.ShapeDtypeStruct((cx, band, nz), f32),
        in_specs=[anyw] * 11,
        out_specs=vmem,
        scratch_shapes=[
            pltpu.VMEM((levels, lx + 2 * H, ly + 2 * PAD, nz), f32),
            pltpu.VMEM((lx, ly, nz), f32),
            pltpu.VMEM((cx, band, nz), f32),
            pltpu.VMEM((steps, lx, ly, nz), f32),
            pltpu.VMEM((steps, lx, ly, nz), f32),
            pltpu.VMEM((lx, ly, nz), f32),
            pltpu.VMEM((lx, ly, nz), f32),
            pltpu.VMEM((lx, band, nz), f32),
            pltpu.VMEM((lx, band, nz), f32),
            pltpu.VMEM((2, cx, band, nz), f32),
            dma((levels, 2 * (ly // CHUNK) + 1)),
            dma((levels, 2 * (ly // CHUNK) + 1)),
            dma((2, cx)),
            dma((2, cx)),
            dma((13,)),
            dma((steps,)),
            dma((3,)),
            dma((3,)),
        ],
        compiler_params=pltpu.CompilerParams(
            collective_id=0, has_side_effects=True, vmem_limit_bytes=60 * 2**20
        ),
        name="waves",
    )(velocity, wave_now, wave_prev, adjoint_now, adjoint_prev, far, same, cross, s_f, o_f, m_f)


def solution(mesh):
    in_specs = (
        P("space", None, None),
        P("shot", "space", None, None),
        P("shot", "space", None, None),
        P("shot", "space", None, None),
        P("shot", "space", None, None),
        P("shot", None),
        P("shot", None, None),
        P("space"),
        P("space"),
        P("shot", None, "space"),
    )
    out_specs = P("space", "shot", None)
    return jax.shard_map(
        per_device, mesh=mesh, in_specs=in_specs, out_specs=out_specs, check_vma=False
    )
```

```python
import functools

import jax
import jax.numpy as jnp
from jax import lax
from jax.experimental import pallas as pl
from jax.experimental.pallas import tpu as pltpu
from jax.sharding import PartitionSpec as P

TAPS = (-205.0 / 72.0, 8.0 / 5.0, -1.0 / 5.0, 8.0 / 315.0, -1.0 / 560.0)
COURANT = 0.09
MESH = pl.DeviceIdType.MESH
PAD = 8
H = 4
TROWS = 21
CHUNK = 24
PIECE = 48


def scatter_kernel(
    enc, senc, vals, svals, s_out, o_out, m_out, low, high, s_v, o_v, m_v, sems
):
    steps, lx, ly, lz = s_v.shape
    half = lx // 2
    slots = enc.shape[1]
    lane = lax.broadcasted_iota(jnp.int32, (8, lz), 1)

    def clear(i, _):
        at = pl.ds(pl.multiple_of(i * 64, 8), 64)
        low[at, :] = jnp.zeros((64, lz), jnp.float32)
        high[at, :] = jnp.zeros((64, lz), jnp.float32)
        return 0

    lax.fori_loop(0, low.shape[0] // 64, clear, 0)

    def place(cells, values, first, tiles):
        def one(j, _):
            places = []
            for h, table in enumerate((low, high)):
                cell = cells[h, first + j]
                line = lax.shift_right_logical(cell, 7)
                z = cell & 127
                shift = (z - j) & 127
                here = lane == z
                for k, tile in enumerate(tiles):
                    value = values[h % values.shape[0], 8 * k : 8 * k + 8, first : first + 128]
                    at = pl.ds(line * TROWS + 8 * tile, 8)
                    added = jnp.where(here, pltpu.roll(value, shift, 1), 0.0)
                    places.append((table, at, table[at, :] + added))
            for table, at, value in places:
                table[at, :] = value
            return 0

        lax.fori_loop(0, 128, one, 0, unroll=8)

    for first in range(0, slots, 128):
        place(enc, vals, first, (0, 1))
    for first in range(0, senc.shape[1], 128):
        place(senc, svals, first, (1, 2))

    def copies(xi):
        return (
            pltpu.make_async_copy(s_v.at[:, xi], s_out.at[:, xi], sems.at[0, xi]),
            pltpu.make_async_copy(o_v.at[:, xi], o_out.at[:, xi], sems.at[1, xi]),
            pltpu.make_async_copy(m_v.at[xi], m_out.at[xi], sems.at[2, xi]),
        )

    for h, table in enumerate((low, high)):

        def spread(x0, _):
            xi = x0 + half * h
            for y0 in range(0, ly, 8):
                base = (x0 * ly + y0) * TROWS
                for t in range(steps):
                    o_v[t, xi, y0 : y0 + 8, :] = table[pl.ds(base + t, 8, stride=TROWS), :]
                    s_v[t, xi, y0 : y0 + 8, :] = table[pl.ds(base + 11 + t, 8, stride=TROWS), :]
                m_v[xi, y0 : y0 + 8, :] = table[pl.ds(base + 10, 8, stride=TROWS), :]
            for copy in copies(xi):
                copy.start()
            return 0

        lax.fori_loop(0, half, spread, 0)

    def finish(xi, _):
        for copy in copies(xi):
            copy.wait()
        return 0

    lax.fori_loop(0, lx, finish, 0)


def wave_kernel(
    vel, now, prev, adj, adjp, far, same, cross, s_hbm, o_hbm, m_hbm, out,
    u, c2, s_v, o_v, m_v, img, pair, red, got,
    halo_send, halo_recv, adj_send, adj_recv, loc, s_sem, red_send, red_recv,
):
    cx, ny, nz = vel.shape
    lx, ly = 2 * cx, ny // 2
    steps = s_hbm.shape[0]
    n_space = lax.axis_size("space")
    i = lax.axis_index("space")
    s = lax.axis_index("shot")
    a, b = i // 2, i % 2
    x, core = s // 2, s % 2
    has_low = a > 0
    has_high = a < n_space // 2 - 1
    other_i = i + 1 - 2 * b
    other_s = s + 1 - 2 * core
    cross_s = s + 2 - 4 * x
    top = 2 * steps + 3

    def zero_low(l, _):
        u[l, 0:H, PAD : PAD + ly, :] = jnp.zeros((H, ly, nz), jnp.float32)
        return 0

    def zero_high(l, _):
        u[l, H + lx : lx + 2 * H, PAD : PAD + ly, :] = jnp.zeros((H, ly, nz), jnp.float32)
        return 0

    def zero_left(l, _):
        u[l, H : H + lx, 0:PAD, :] = jnp.zeros((lx, PAD, nz), jnp.float32)
        return 0

    def zero_right(l, _):
        u[l, H : H + lx, PAD + ly : 2 * PAD + ly, :] = jnp.zeros((lx, PAD, nz), jnp.float32)
        return 0

    @pl.when(jnp.logical_not(has_low))
    def _():
        lax.fori_loop(0, top, zero_low, 0)

    @pl.when(jnp.logical_not(has_high))
    def _():
        lax.fori_loop(0, top, zero_high, 0)

    @pl.when(b == 0)
    def _():
        lax.fori_loop(0, top, zero_left, 0)

    @pl.when(b == 1)
    def _():
        lax.fori_loop(0, top, zero_right, 0)

    level_of = (1, None, 0, steps + 3, steps + 2)
    sources = (now, vel, prev, adj, adjp)
    mine = pl.ds(pl.multiple_of(ly * b, 8), ly)
    theirs = pl.ds(pl.multiple_of(ly * (1 - b), 8), ly)

    def landing(k, half):
        if level_of[k] is None:
            return c2.at[pl.ds(cx * half, cx)]
        return u.at[level_of[k], pl.ds(H + cx * half, cx), PAD : PAD + ly, :]

    def view(k, rows):
        if k == 1:
            return sources[k].at[:, rows, :]
        return sources[k].at[0, :, rows, :]

    def local_copy(k):
        return pltpu.make_async_copy(view(k, mine), landing(k, b), loc.at[k])

    def far_copy(k):
        return pltpu.make_async_copy(far.at[k], landing(k, 1 - b), loc.at[8 + k])

    def low_copy(first):
        return pltpu.make_async_copy(first, u.at[1, 0:H, PAD : PAD + ly, :], loc.at[11])

    def high_copy(first):
        return pltpu.make_async_copy(
            first, u.at[1, H + lx : lx + 2 * H, PAD : PAD + ly, :], loc.at[12]
        )

    def s_copy(k):
        return pltpu.make_async_copy(s_hbm.at[k], s_v.at[k], s_sem.at[k])

    def partner_layer(k, layer):
        return pltpu.make_async_remote_copy(
            src_ref=sources[k].at[0, layer, theirs, :],
            dst_ref=u.at[level_of[k], H + cx * b + layer, PAD : PAD + ly, :],
            send_sem=adj_send.at[k - 3, layer], recv_sem=adj_recv.at[k - 3, layer],
            device_id=(other_i, s), device_id_type=MESH,
        )

    extra = [
        pltpu.make_async_copy(m_hbm, m_v, loc.at[5]),
        pltpu.make_async_copy(o_hbm, o_v, loc.at[7]),
    ]

    def each_edge(call):
        for parity, low, high in ((0, cross, same), (1, same, cross)):

            @pl.when(jnp.logical_and(b == parity, has_low))
            def _():
                call(low_copy(low))

            @pl.when(jnp.logical_and(b == parity, has_high))
            def _():
                call(high_copy(high))

    for k in range(3):
        local_copy(k).start()
        far_copy(k).start()
    each_edge(lambda copy: copy.start())
    for k in range(steps):
        s_copy(k).start()
    for k in (3, 4):
        local_copy(k).start()
    for copy in extra:
        copy.start()

    barrier = pltpu.get_barrier_semaphore()
    for target in ((other_i, s), (i, other_s), (i, cross_s), (other_i, cross_s)):
        pl.semaphore_signal(barrier, inc=1, device_id=target, device_id_type=MESH)

    @pl.when(has_low)
    def _():
        pl.semaphore_signal(barrier, inc=1, device_id=(i - 2, s), device_id_type=MESH)

    @pl.when(has_high)
    def _():
        pl.semaphore_signal(barrier, inc=1, device_id=(i + 2, s), device_id_type=MESH)

    pl.semaphore_wait(barrier, 4 + has_low.astype(jnp.int32) + has_high.astype(jnp.int32))


    pieces = ly // PIECE

    def send_up(l, p):
        rows = slice(PAD + PIECE * p, PAD + PIECE * (p + 1))
        return pltpu.make_async_remote_copy(
            src_ref=u.at[l, lx : lx + H, rows, :],
            dst_ref=u.at[l, 0:H, rows, :],
            send_sem=halo_send.at[l, p], recv_sem=halo_recv.at[l, p],
            device_id=(i + 2, s), device_id_type=MESH,
        )

    def send_down(l, p):
        rows = slice(PAD + PIECE * p, PAD + PIECE * (p + 1))
        return pltpu.make_async_remote_copy(
            src_ref=u.at[l, H : 2 * H, rows, :],
            dst_ref=u.at[l, lx + H : lx + 2 * H, rows, :],
            send_sem=halo_send.at[l, pieces + p], recv_sem=halo_recv.at[l, pieces + p],
            device_id=(i - 2, s), device_id_type=MESH,
        )

    def send_side(l):
        return pltpu.make_async_remote_copy(
            src_ref=u.at[l, H : H + lx, pl.ds(pl.multiple_of(ly - (ly - PAD) * b, 8), PAD), :],
            dst_ref=u.at[l, H : H + lx, pl.ds(pl.multiple_of((ly + PAD) * b, 8), PAD), :],
            send_sem=halo_send.at[l, 2 * pieces], recv_sem=halo_recv.at[l, 2 * pieces],
            device_id=(other_i, s), device_id_type=MESH,
        )

    def start_down(l, p):
        @pl.when(has_low)
        def _():
            send_down(l, p).start()

    def start_up(l, p):
        @pl.when(has_high)
        def _():
            send_up(l, p).start()

    def start_all(l, order):
        send_side(l).start()
        for p in order:
            start_down(l, p)
            start_up(l, p)

    def wait_low(l, p, arrives):
        @pl.when(jnp.logical_and(has_low, arrives))
        def _():
            send_up(l, p).wait_recv()
            send_down(l, p).wait_send()

    def wait_high(l, p, arrives):
        @pl.when(jnp.logical_and(has_high, arrives))
        def _():
            send_down(l, p).wait_recv()
            send_up(l, p).wait_send()

    def settle(k):
        local_copy(k).wait()
        far_copy(k).wait()

    lane = lax.broadcasted_iota(jnp.int32, (CHUNK, nz), 1)

    def laplace(l, xi, r0):
        rows = lambda d: slice(PAD + r0 + d, PAD + r0 + d + CHUNK)
        centre = u[l, H + xi, rows(0), :]
        up = lambda v, k: jnp.where(lane >= k, pltpu.roll(v, k, 1), 0.0)
        down = lambda v, k: jnp.where(lane < nz - k, pltpu.roll(v, nz - k, 1), 0.0)
        up1, up2, down1, down2 = up(centre, 1), up(centre, 2), down(centre, 1), down(centre, 2)
        along = {1: up1 + down1, 2: up2 + down2}
        result = 3.0 * TAPS[0] * centre
        for k in range(1, H + 1):
            beside = u[l, H + xi + k, rows(0), :] + u[l, H + xi - k, rows(0), :]
            beside = beside + (u[l, H + xi, rows(k), :] + u[l, H + xi, rows(-k), :])
            if k in along:
                beside = beside + along[k]
            result = result + TAPS[k] * beside
        result = result + up(TAPS[3] * up1 + TAPS[4] * up2, 2)
        result = result + down(TAPS[3] * down1 + TAPS[4] * down2, 2)
        return centre, result

    def sweep(first, last, p, body):
        def layer(xi, _):
            for r0 in range(PIECE * p, PIECE * (p + 1), CHUNK):
                body(xi, r0)
            return 0

        lax.fori_loop(first, last, layer, 0)

    def step(cur, arrives, more, order, cell):
        for n, p in enumerate(order):
            if n == 0:
                send_side(cur).wait()
            wait_low(cur, p, arrives)
            sweep(0, H, p, cell)

            @pl.when(more)
            def _():
                start_down(cur + 1, p)

            wait_high(cur, p, arrives)
            sweep(lx - H, lx, p, cell)

            @pl.when(more)
            def _():
                start_up(cur + 1, p)

            sweep(H, lx - H, p, cell)
            if n == 0:

                @pl.when(more)
                def _():
                    send_side(cur + 1).start()

    def square(xi, r0):
        value = COURANT * c2[xi, r0 : r0 + CHUNK, :]
        c2[xi, r0 : r0 + CHUNK, :] = value * value
        img[xi, r0 : r0 + CHUNK, :] = jnp.zeros((CHUNK, nz), jnp.float32)

    def forward(order, t, _):
        cur = t + 1

        def cell(xi, r0):
            rows = slice(PAD + r0, PAD + r0 + CHUNK)
            inner = slice(r0, r0 + CHUNK)
            centre, lap = laplace(cur, xi, r0)
            fresh = 2.0 * centre - u[t, H + xi, rows, :] + c2[xi, inner, :] * lap
            u[t + 2, H + xi, rows, :] = fresh + s_v[t, xi, inner, :]

        @pl.when(t < cx)
        def _():
            partner_layer(3, t).start()
            partner_layer(4, t).start()

        s_copy(t).wait()
        step(cur, t > 0, t < steps - 1, order, cell)

        @pl.when(t == steps - 2)
        def _():
            for k in (3, 4):
                local_copy(k).wait()

                def arrive(layer, _):
                    partner_layer(k, layer).wait()
                    return 0

                lax.fori_loop(0, cx, arrive, 0)
            start_all(steps + 3, order)

        return 0

    def backward(order, k, _):
        t = steps - 1 - k
        cur = steps + 3 + k

        def cell(xi, r0):
            rows = slice(PAD + r0, PAD + r0 + CHUNK)
            inner = slice(r0, r0 + CHUNK)
            centre, lap = laplace(cur, xi, r0)
            fresh = 2.0 * centre - u[cur - 1, H + xi, rows, :] + c2[xi, inner, :] * lap
            later = u[t + 2, H + xi, rows, :]
            fresh = fresh + m_v[xi, inner, :] * (later - o_v[t, xi, inner, :])
            accel = later - 2.0 * u[t + 1, H + xi, rows, :] + u[t, H + xi, rows, :]
            img[xi, inner, :] = img[xi, inner, :] + fresh * accel
            u[cur + 1, H + xi, rows, :] = fresh

        step(cur, True, k < steps - 1, order, cell)
        return 0

    def both(order):
        settle(0)
        send_side(1).start()
        settle(1)
        for p in order:
            sweep(0, lx, p, square)
        settle(2)
        each_edge(lambda copy: copy.wait())
        lax.fori_loop(0, steps, functools.partial(forward, order), 0)
        for copy in extra:
            copy.wait()
        lax.fori_loop(0, steps, functools.partial(backward, order), 0)

    @pl.when(b == 0)
    def _():
        both(tuple(range(pieces - 1, -1, -1)))

    @pl.when(b == 1)
    def _():
        both(tuple(range(pieces)))

    band = out.shape[1]
    keep = pl.multiple_of(band * core, 8)
    give = pl.multiple_of(band * (1 - core), 8)
    swap = pltpu.make_async_remote_copy(
        src_ref=img.at[:, pl.ds(give, band), :], dst_ref=pair,
        send_sem=red_send.at[2], recv_sem=red_recv.at[2],
        device_id=(i, other_s), device_id_type=MESH,
    )
    swap.start()
    swap.wait()

    def add_pair(xi, _):
        red[xi] = img[xi, pl.ds(keep, band), :] + pair[xi]
        return 0

    lax.fori_loop(0, lx, add_pair, 0)

    def deliver(target):
        return pltpu.make_async_remote_copy(
            src_ref=red.at[pl.ds(cx * target, cx)], dst_ref=got.at[x],
            send_sem=red_send.at[target], recv_sem=red_recv.at[x],
            device_id=(2 * a + target, 2 * b + core), device_id_type=MESH,
        )

    def arrival(k):
        return pltpu.make_async_remote_copy(
            src_ref=red.at[0:cx], dst_ref=got.at[k],
            send_sem=red_send.at[k], recv_sem=red_recv.at[k],
            device_id=(other_i, s), device_id_type=MESH,
        )

    for target in range(2):
        own = jnp.logical_and(x == b, b == target)

        @pl.when(jnp.logical_not(own))
        def _():
            deliver(target).start()

        @pl.when(own)
        def _():
            got[target] = red[cx * target : cx * (target + 1)]

    for k in range(2):
        own = jnp.logical_and(x == b, x == k)

        @pl.when(jnp.logical_not(own))
        def _():
            arrival(k).wait_recv()
            deliver(k).wait_send()

    for xi in range(cx):
        out[xi] = got[0, xi] + got[1, xi]


def per_device(
    velocity, wave_now, wave_prev, adjoint_now, adjoint_prev,
    source_cells, wavelet, receiver_cells, receiver_counts, observed,
):
    cx, ny, nz = velocity.shape
    lx, ly = 2 * cx, ny // 2
    lines = lx * ly
    steps = wavelet.shape[1]
    slots = receiver_cells.shape[0]
    count = lax.axis_size("space")
    i = lax.axis_index("space")
    a, b = i // 2, i % 2
    swap = [(j, j + 1 - 2 * (j % 2)) for j in range(count)]

    live = jnp.arange(slots, dtype=jnp.int32) < receiver_counts[0]
    own_cells = jnp.where(live, receiver_cells, -1)
    their_cells = lax.ppermute(own_cells, "space", swap)
    their_obs = lax.ppermute(observed[0], "space", swap)

    def rows_of(block, part):
        return lax.dynamic_slice_in_dim(block, ly * part, ly, 1)

    far = jnp.stack([rows_of(f, 1 - b) for f in (wave_now[0], velocity, wave_prev[0])])
    far = lax.ppermute(far, "space", swap)
    edge = lax.dynamic_slice_in_dim(wave_now[0], (cx - H) * b, H, 0)
    beyond = [(j, j + 4 * (j % 2) - 2) for j in range(count)]
    across = [(j, j + 2 * (j % 2) - 1) for j in range(count)]
    within = lambda pairs: [(j, k) for j, k in pairs if 0 <= k < count]
    same = lax.ppermute(rows_of(edge, b), "space", within(beyond))
    cross = lax.ppermute(rows_of(edge, 1 - b), "space", within(across))

    def code(cells, layer0, layers):
        line = cells // nz
        xg = line // ny + layer0
        yl = line % ny - ly * b
        ok = (cells >= 0) & (xg >= 0) & (xg < layers) & (yl >= 0) & (yl < ly)
        return jnp.where(ok, (xg * ly + yl) * nz + cells % nz, lines // 2 * nz)

    first = b == 0
    enc = code(
        jnp.stack([jnp.where(first, own_cells, their_cells), jnp.where(first, their_cells, own_cells)]),
        0, cx,
    )
    senc = jnp.stack([code(source_cells[0], -lx * a - cx * h, cx) for h in range(2)])
    vals = jnp.stack(
        [jnp.where(first, observed[0], their_obs), jnp.where(first, their_obs, observed[0])]
    )
    ones = jnp.ones((2, 1, slots), jnp.float32)
    vals = jnp.concatenate([vals, ones, jnp.zeros((2, 5, slots), jnp.float32)], axis=1)
    w = wavelet[0]
    gap = jnp.zeros((3, w.shape[1]), jnp.float32)
    svals = jnp.concatenate([gap, w, gap], axis=0)[None]

    smem = pl.BlockSpec(memory_space=pltpu.SMEM)
    vmem = pl.BlockSpec(memory_space=pltpu.VMEM)
    anyw = pl.BlockSpec(memory_space=pl.ANY)
    f32 = jnp.float32
    dense = jax.ShapeDtypeStruct((steps, lx, ly, nz), f32)
    field = jax.ShapeDtypeStruct((lx, ly, nz), f32)
    s_f, o_f, m_f = pl.pallas_call(
        scatter_kernel,
        out_shape=(dense, dense, field),
        in_specs=[smem, smem, vmem, vmem],
        out_specs=(anyw, anyw, anyw),
        scratch_shapes=[
            pltpu.VMEM(((lines // 2 + 64) * TROWS, nz), f32),
            pltpu.VMEM(((lines // 2 + 64) * TROWS, nz), f32),
            pltpu.VMEM((steps, lx, ly, nz), f32),
            pltpu.VMEM((steps, lx, ly, nz), f32),
            pltpu.VMEM((lx, ly, nz), f32),
            pltpu.SemaphoreType.DMA((3, lx)),
        ],
        compiler_params=pltpu.CompilerParams(vmem_limit_bytes=48 * 2**20),
        cost_estimate=pl.CostEstimate(flops=10**9, bytes_accessed=80 * 10**6, transcendentals=0),
        name="scatter",
    )(enc, senc, vals, svals)

    levels = 2 * steps + 4
    band = ny // 4
    dma = pltpu.SemaphoreType.DMA
    image = pl.pallas_call(
        wave_kernel,
        out_shape=jax.ShapeDtypeStruct((cx, band, nz), f32),
        in_specs=[anyw] * 11,
        out_specs=vmem,
        scratch_shapes=[
            pltpu.VMEM((levels, lx + 2 * H, ly + 2 * PAD, nz), f32),
            pltpu.VMEM((lx, ly, nz), f32),
            pltpu.VMEM((steps, lx, ly, nz), f32),
            pltpu.VMEM((steps, lx, ly, nz), f32),
            pltpu.VMEM((lx, ly, nz), f32),
            pltpu.VMEM((lx, ly, nz), f32),
            pltpu.VMEM((lx, band, nz), f32),
            pltpu.VMEM((lx, band, nz), f32),
            pltpu.VMEM((2, cx, band, nz), f32),
            dma((levels, 2 * (ly // PIECE) + 1)),
            dma((levels, 2 * (ly // PIECE) + 1)),
            dma((2, cx)),
            dma((2, cx)),
            dma((13,)),
            dma((steps,)),
            dma((3,)),
            dma((3,)),
        ],
        compiler_params=pltpu.CompilerParams(
            collective_id=0, has_side_effects=True, vmem_limit_bytes=60 * 2**20
        ),
        name="waves",
    )(velocity, wave_now, wave_prev, adjoint_now, adjoint_prev, far, same, cross, s_f, o_f, m_f)
    own = lax.dynamic_slice_in_dim(velocity, lax.axis_index("shot") * band, band, 1)
    return -2.0 / (own * own * own) * image


def solution(mesh):
    in_specs = (
        P("space", None, None),
        P("shot", "space", None, None),
        P("shot", "space", None, None),
        P("shot", "space", None, None),
        P("shot", "space", None, None),
        P("shot", None),
        P("shot", None, None),
        P("space"),
        P("space"),
        P("shot", None, "space"),
    )
    out_specs = P("space", "shot", None)
    return jax.shard_map(
        per_device, mesh=mesh, in_specs=in_specs, out_specs=out_specs, check_vma=False
    )
```

```python
import functools

import jax
import jax.numpy as jnp
from jax import lax
from jax.experimental import pallas as pl
from jax.experimental.pallas import tpu as pltpu
from jax.sharding import PartitionSpec as P

TAPS = (-205.0 / 72.0, 8.0 / 5.0, -1.0 / 5.0, 8.0 / 315.0, -1.0 / 560.0)
COURANT = 0.09
MESH = pl.DeviceIdType.MESH
PAD = 8
H = 4
TROWS = 21
CHUNK = 32
PIECE = 32
GROUP = 4


def scatter_kernel(
    enc, senc, vals, svals, s_out, o_out, m_out, low, high, s_v, o_v, m_v, sems
):
    steps, lx, ly, lz = s_v.shape
    half = lx // 2
    slots = enc.shape[1]
    lane = lax.broadcasted_iota(jnp.int32, (8, lz), 1)

    def clear(i, _):
        at = pl.ds(pl.multiple_of(i * 64, 8), 64)
        low[at, :] = jnp.zeros((64, lz), jnp.float32)
        high[at, :] = jnp.zeros((64, lz), jnp.float32)
        return 0

    lax.fori_loop(0, low.shape[0] // 64, clear, 0)

    def place(cells, values, first, tiles):
        def one(j, _):
            places = []
            for h, table in enumerate((low, high)):
                cell = cells[h, first + j]
                line = lax.shift_right_logical(cell, 7)
                z = cell & 127
                shift = (z - j) & 127
                here = lane == z
                for k, tile in enumerate(tiles):
                    value = values[h % values.shape[0], 8 * k : 8 * k + 8, first : first + 128]
                    at = pl.ds(line * TROWS + 8 * tile, 8)
                    added = jnp.where(here, pltpu.roll(value, shift, 1), 0.0)
                    places.append((table, at, table[at, :] + added))
            for table, at, value in places:
                table[at, :] = value
            return 0

        lax.fori_loop(0, 128, one, 0, unroll=8)

    for first in range(0, slots, 128):
        place(enc, vals, first, (0, 1))
    for first in range(0, senc.shape[1], 128):
        place(senc, svals, first, (1, 2))

    def copies(xi):
        return (
            pltpu.make_async_copy(s_v.at[:, xi], s_out.at[:, xi], sems.at[0, xi]),
            pltpu.make_async_copy(o_v.at[:, xi], o_out.at[:, xi], sems.at[1, xi]),
            pltpu.make_async_copy(m_v.at[xi], m_out.at[xi], sems.at[2, xi]),
        )

    for h, table in enumerate((low, high)):

        def spread(x0, _):
            xi = x0 + half * h
            for y0 in range(0, ly, 8):
                base = (x0 * ly + y0) * TROWS
                for t in range(steps):
                    o_v[t, xi, y0 : y0 + 8, :] = table[pl.ds(base + t, 8, stride=TROWS), :]
                    s_v[t, xi, y0 : y0 + 8, :] = table[pl.ds(base + 11 + t, 8, stride=TROWS), :]
                m_v[xi, y0 : y0 + 8, :] = table[pl.ds(base + 10, 8, stride=TROWS), :]
            for copy in copies(xi):
                copy.start()
            return 0

        lax.fori_loop(0, half, spread, 0)

    def finish(xi, _):
        for copy in copies(xi):
            copy.wait()
        return 0

    lax.fori_loop(0, lx, finish, 0)


def wave_kernel(
    vel, now, prev, adj, adjp, far, same, cross, s_hbm, o_hbm, m_hbm, out,
    u, c2, s_v, o_v, m_v, img, pair, red, got,
    halo_send, halo_recv, adj_send, adj_recv, loc, s_sem, red_send, red_recv,
):
    cx, ny, nz = vel.shape
    lx, ly = 2 * cx, ny // 2
    steps = s_hbm.shape[0]
    n_space = lax.axis_size("space")
    i = lax.axis_index("space")
    s = lax.axis_index("shot")
    a, b = i // 2, i % 2
    x, core = s // 2, s % 2
    has_low = a > 0
    has_high = a < n_space // 2 - 1
    other_i = i + 1 - 2 * b
    other_s = s + 1 - 2 * core
    cross_s = s + 2 - 4 * x
    top = 2 * steps + 3

    def zero_low(l, _):
        u[l, 0:H, PAD : PAD + ly, :] = jnp.zeros((H, ly, nz), jnp.float32)
        return 0

    def zero_high(l, _):
        u[l, H + lx : lx + 2 * H, PAD : PAD + ly, :] = jnp.zeros((H, ly, nz), jnp.float32)
        return 0

    def zero_left(l, _):
        u[l, H : H + lx, 0:PAD, :] = jnp.zeros((lx, PAD, nz), jnp.float32)
        return 0

    def zero_right(l, _):
        u[l, H : H + lx, PAD + ly : 2 * PAD + ly, :] = jnp.zeros((lx, PAD, nz), jnp.float32)
        return 0

    @pl.when(jnp.logical_not(has_low))
    def _():
        lax.fori_loop(0, top, zero_low, 0)

    @pl.when(jnp.logical_not(has_high))
    def _():
        lax.fori_loop(0, top, zero_high, 0)

    @pl.when(b == 0)
    def _():
        lax.fori_loop(0, top, zero_left, 0)

    @pl.when(b == 1)
    def _():
        lax.fori_loop(0, top, zero_right, 0)

    level_of = (1, None, 0, steps + 3, steps + 2)
    sources = (now, vel, prev, adj, adjp)
    mine = pl.ds(pl.multiple_of(ly * b, 8), ly)
    theirs = pl.ds(pl.multiple_of(ly * (1 - b), 8), ly)

    def landing(k, half):
        if level_of[k] is None:
            return c2.at[pl.ds(cx * half, cx)]
        return u.at[level_of[k], pl.ds(H + cx * half, cx), PAD : PAD + ly, :]

    def view(k, rows):
        if k == 1:
            return sources[k].at[:, rows, :]
        return sources[k].at[0, :, rows, :]

    def local_copy(k):
        return pltpu.make_async_copy(view(k, mine), landing(k, b), loc.at[k])

    def far_copy(k):
        return pltpu.make_async_copy(far.at[k], landing(k, 1 - b), loc.at[8 + k])

    def low_copy(first):
        return pltpu.make_async_copy(first, u.at[1, 0:H, PAD : PAD + ly, :], loc.at[11])

    def high_copy(first):
        return pltpu.make_async_copy(
            first, u.at[1, H + lx : lx + 2 * H, PAD : PAD + ly, :], loc.at[12]
        )

    def s_copy(k):
        return pltpu.make_async_copy(s_hbm.at[k], s_v.at[k], s_sem.at[k])

    def partner_layer(k, layer):
        return pltpu.make_async_remote_copy(
            src_ref=sources[k].at[0, layer, theirs, :],
            dst_ref=u.at[level_of[k], H + cx * b + layer, PAD : PAD + ly, :],
            send_sem=adj_send.at[k - 3, layer], recv_sem=adj_recv.at[k - 3, layer],
            device_id=(other_i, s), device_id_type=MESH,
        )

    extra = [
        pltpu.make_async_copy(m_hbm, m_v, loc.at[5]),
        pltpu.make_async_copy(o_hbm, o_v, loc.at[7]),
    ]

    def each_edge(call):
        for parity, low, high in ((0, cross, same), (1, same, cross)):

            @pl.when(jnp.logical_and(b == parity, has_low))
            def _():
                call(low_copy(low))

            @pl.when(jnp.logical_and(b == parity, has_high))
            def _():
                call(high_copy(high))

    for k in range(3):
        local_copy(k).start()
        far_copy(k).start()
    each_edge(lambda copy: copy.start())
    for k in range(steps):
        s_copy(k).start()
    for k in (3, 4):
        local_copy(k).start()
    for copy in extra:
        copy.start()

    barrier = pltpu.get_barrier_semaphore()
    for target in ((other_i, s), (i, other_s), (i, cross_s), (other_i, cross_s)):
        pl.semaphore_signal(barrier, inc=1, device_id=target, device_id_type=MESH)

    @pl.when(has_low)
    def _():
        pl.semaphore_signal(barrier, inc=1, device_id=(i - 2, s), device_id_type=MESH)

    @pl.when(has_high)
    def _():
        pl.semaphore_signal(barrier, inc=1, device_id=(i + 2, s), device_id_type=MESH)

    pl.semaphore_wait(barrier, 4 + has_low.astype(jnp.int32) + has_high.astype(jnp.int32))


    pieces = ly // PIECE

    def send_up(l, p):
        rows = slice(PAD + PIECE * p, PAD + PIECE * (p + 1))
        return pltpu.make_async_remote_copy(
            src_ref=u.at[l, lx : lx + H, rows, :],
            dst_ref=u.at[l, 0:H, rows, :],
            send_sem=halo_send.at[l, p], recv_sem=halo_recv.at[l, p],
            device_id=(i + 2, s), device_id_type=MESH,
        )

    def send_down(l, p):
        rows = slice(PAD + PIECE * p, PAD + PIECE * (p + 1))
        return pltpu.make_async_remote_copy(
            src_ref=u.at[l, H : 2 * H, rows, :],
            dst_ref=u.at[l, lx + H : lx + 2 * H, rows, :],
            send_sem=halo_send.at[l, pieces + p], recv_sem=halo_recv.at[l, pieces + p],
            device_id=(i - 2, s), device_id_type=MESH,
        )

    def send_side(l):
        return pltpu.make_async_remote_copy(
            src_ref=u.at[l, H : H + lx, pl.ds(pl.multiple_of(ly - (ly - PAD) * b, 8), PAD), :],
            dst_ref=u.at[l, H : H + lx, pl.ds(pl.multiple_of((ly + PAD) * b, 8), PAD), :],
            send_sem=halo_send.at[l, 2 * pieces], recv_sem=halo_recv.at[l, 2 * pieces],
            device_id=(other_i, s), device_id_type=MESH,
        )

    def start_down(l, p):
        @pl.when(has_low)
        def _():
            send_down(l, p).start()

    def start_up(l, p):
        @pl.when(has_high)
        def _():
            send_up(l, p).start()

    def start_all(l, order):
        send_side(l).start()
        for p in order:
            start_down(l, p)
            start_up(l, p)

    def wait_low(l, p, arrives):
        @pl.when(jnp.logical_and(has_low, arrives))
        def _():
            send_up(l, p).wait_recv()
            send_down(l, p).wait_send()

    def wait_high(l, p, arrives):
        @pl.when(jnp.logical_and(has_high, arrives))
        def _():
            send_down(l, p).wait_recv()
            send_up(l, p).wait_send()

    def settle(k):
        local_copy(k).wait()
        far_copy(k).wait()

    lane = lax.broadcasted_iota(jnp.int32, (CHUNK, nz), 1)

    def laplace(l, xi, r0):
        rows = lambda d: slice(PAD + r0 + d, PAD + r0 + d + CHUNK)
        centre = u[l, H + xi, rows(0), :]
        result = 3.0 * TAPS[0] * centre
        for k in range(1, H + 1):
            beside = u[l, H + xi + k, rows(0), :] + u[l, H + xi - k, rows(0), :]
            beside = beside + (u[l, H + xi, rows(k), :] + u[l, H + xi, rows(-k), :])
            above = jnp.where(lane < nz - k, pltpu.roll(centre, nz - k, 1), 0.0)
            below = jnp.where(lane >= k, pltpu.roll(centre, k, 1), 0.0)
            result = result + TAPS[k] * (beside + (above + below))
        return centre, result

    def sweep(first, last, p, body):
        def group(g, _):
            writes = []
            for j in range(GROUP):
                writes += body(first + g * GROUP + j, PIECE * p)
            for ref, at, value in writes:
                ref[at] = value
            return 0

        count = (last - first) // GROUP
        if count == 1:
            group(0, 0)
        else:
            lax.fori_loop(0, count, group, 0)

    def step(cur, arrives, more, order, cell):
        for n, p in enumerate(order):
            if n == 0:
                send_side(cur).wait()
            wait_low(cur, p, arrives)
            sweep(0, H, p, cell)

            @pl.when(more)
            def _():
                start_down(cur + 1, p)

            wait_high(cur, p, arrives)
            sweep(lx - H, lx, p, cell)

            @pl.when(more)
            def _():
                start_up(cur + 1, p)

            sweep(H, lx - H, p, cell)
            if n == 0:

                @pl.when(more)
                def _():
                    send_side(cur + 1).start()

    def square(xi, r0):
        value = COURANT * c2[xi, r0 : r0 + CHUNK, :]
        at = (xi, slice(r0, r0 + CHUNK))
        return [(c2, at, value * value), (img, at, jnp.zeros((CHUNK, nz), jnp.float32))]

    def forward(order, t, _):
        cur = t + 1

        def cell(xi, r0):
            rows = slice(PAD + r0, PAD + r0 + CHUNK)
            inner = slice(r0, r0 + CHUNK)
            centre, lap = laplace(cur, xi, r0)
            fresh = 2.0 * centre - u[t, H + xi, rows, :] + c2[xi, inner, :] * lap
            return [(u, (t + 2, H + xi, rows), fresh + s_v[t, xi, inner, :])]

        @pl.when(t < cx)
        def _():
            partner_layer(3, t).start()
            partner_layer(4, t).start()

        s_copy(t).wait()
        step(cur, t > 0, t < steps - 1, order, cell)

        @pl.when(t == steps - 2)
        def _():
            for k in (3, 4):
                local_copy(k).wait()

                def arrive(layer, _):
                    partner_layer(k, layer).wait()
                    return 0

                lax.fori_loop(0, cx, arrive, 0)
            start_all(steps + 3, order)

        return 0

    def backward(order, k, _):
        t = steps - 1 - k
        cur = steps + 3 + k

        def cell(xi, r0):
            rows = slice(PAD + r0, PAD + r0 + CHUNK)
            inner = slice(r0, r0 + CHUNK)
            centre, lap = laplace(cur, xi, r0)
            fresh = 2.0 * centre - u[cur - 1, H + xi, rows, :] + c2[xi, inner, :] * lap
            later = u[t + 2, H + xi, rows, :]
            fresh = fresh + m_v[xi, inner, :] * (later - o_v[t, xi, inner, :])
            accel = later - 2.0 * u[t + 1, H + xi, rows, :] + u[t, H + xi, rows, :]
            total = img[xi, inner, :] + fresh * accel
            return [(img, (xi, inner), total), (u, (cur + 1, H + xi, rows), fresh)]

        step(cur, True, k < steps - 1, order, cell)
        return 0

    def both(order):
        settle(0)
        send_side(1).start()
        settle(1)
        for p in order:
            sweep(0, lx, p, square)
        settle(2)
        each_edge(lambda copy: copy.wait())
        lax.fori_loop(0, steps, functools.partial(forward, order), 0)
        for copy in extra:
            copy.wait()
        lax.fori_loop(0, steps, functools.partial(backward, order), 0)

    @pl.when(b == 0)
    def _():
        both(tuple(range(pieces - 1, -1, -1)))

    @pl.when(b == 1)
    def _():
        both(tuple(range(pieces)))

    band = out.shape[1]
    keep = pl.multiple_of(band * core, 8)
    give = pl.multiple_of(band * (1 - core), 8)
    swap = pltpu.make_async_remote_copy(
        src_ref=img.at[:, pl.ds(give, band), :], dst_ref=pair,
        send_sem=red_send.at[2], recv_sem=red_recv.at[2],
        device_id=(i, other_s), device_id_type=MESH,
    )
    swap.start()
    swap.wait()

    def add_pair(xi, _):
        red[xi] = img[xi, pl.ds(keep, band), :] + pair[xi]
        return 0

    lax.fori_loop(0, lx, add_pair, 0)

    def deliver(target):
        return pltpu.make_async_remote_copy(
            src_ref=red.at[pl.ds(cx * target, cx)], dst_ref=got.at[x],
            send_sem=red_send.at[target], recv_sem=red_recv.at[x],
            device_id=(2 * a + target, 2 * b + core), device_id_type=MESH,
        )

    def arrival(k):
        return pltpu.make_async_remote_copy(
            src_ref=red.at[0:cx], dst_ref=got.at[k],
            send_sem=red_send.at[k], recv_sem=red_recv.at[k],
            device_id=(other_i, s), device_id_type=MESH,
        )

    for target in range(2):
        own = jnp.logical_and(x == b, b == target)

        @pl.when(jnp.logical_not(own))
        def _():
            deliver(target).start()

        @pl.when(own)
        def _():
            got[target] = red[cx * target : cx * (target + 1)]

    for k in range(2):
        own = jnp.logical_and(x == b, x == k)

        @pl.when(jnp.logical_not(own))
        def _():
            arrival(k).wait_recv()
            deliver(k).wait_send()

    for xi in range(cx):
        out[xi] = got[0, xi] + got[1, xi]


def per_device(
    velocity, wave_now, wave_prev, adjoint_now, adjoint_prev,
    source_cells, wavelet, receiver_cells, receiver_counts, observed,
):
    cx, ny, nz = velocity.shape
    lx, ly = 2 * cx, ny // 2
    lines = lx * ly
    steps = wavelet.shape[1]
    slots = receiver_cells.shape[0]
    count = lax.axis_size("space")
    i = lax.axis_index("space")
    a, b = i // 2, i % 2
    swap = [(j, j + 1 - 2 * (j % 2)) for j in range(count)]

    live = jnp.arange(slots, dtype=jnp.int32) < receiver_counts[0]
    own_cells = jnp.where(live, receiver_cells, -1)
    their_cells = lax.ppermute(own_cells, "space", swap)
    their_obs = lax.ppermute(observed[0], "space", swap)

    def rows_of(block, part):
        return lax.dynamic_slice_in_dim(block, ly * part, ly, 1)

    far = jnp.stack([rows_of(f, 1 - b) for f in (wave_now[0], velocity, wave_prev[0])])
    far = lax.ppermute(far, "space", swap)
    edge = lax.dynamic_slice_in_dim(wave_now[0], (cx - H) * b, H, 0)
    beyond = [(j, j + 4 * (j % 2) - 2) for j in range(count)]
    across = [(j, j + 2 * (j % 2) - 1) for j in range(count)]
    within = lambda pairs: [(j, k) for j, k in pairs if 0 <= k < count]
    same = lax.ppermute(rows_of(edge, b), "space", within(beyond))
    cross = lax.ppermute(rows_of(edge, 1 - b), "space", within(across))

    def code(cells, layer0, layers):
        line = cells // nz
        xg = line // ny + layer0
        yl = line % ny - ly * b
        ok = (cells >= 0) & (xg >= 0) & (xg < layers) & (yl >= 0) & (yl < ly)
        return jnp.where(ok, (xg * ly + yl) * nz + cells % nz, lines // 2 * nz)

    first = b == 0
    enc = code(
        jnp.stack([jnp.where(first, own_cells, their_cells), jnp.where(first, their_cells, own_cells)]),
        0, cx,
    )
    senc = jnp.stack([code(source_cells[0], -lx * a - cx * h, cx) for h in range(2)])
    vals = jnp.stack(
        [jnp.where(first, observed[0], their_obs), jnp.where(first, their_obs, observed[0])]
    )
    ones = jnp.ones((2, 1, slots), jnp.float32)
    vals = jnp.concatenate([vals, ones, jnp.zeros((2, 5, slots), jnp.float32)], axis=1)
    w = wavelet[0]
    gap = jnp.zeros((3, w.shape[1]), jnp.float32)
    svals = jnp.concatenate([gap, w, gap], axis=0)[None]

    smem = pl.BlockSpec(memory_space=pltpu.SMEM)
    vmem = pl.BlockSpec(memory_space=pltpu.VMEM)
    anyw = pl.BlockSpec(memory_space=pl.ANY)
    f32 = jnp.float32
    dense = jax.ShapeDtypeStruct((steps, lx, ly, nz), f32)
    field = jax.ShapeDtypeStruct((lx, ly, nz), f32)
    s_f, o_f, m_f = pl.pallas_call(
        scatter_kernel,
        out_shape=(dense, dense, field),
        in_specs=[smem, smem, vmem, vmem],
        out_specs=(anyw, anyw, anyw),
        scratch_shapes=[
            pltpu.VMEM(((lines // 2 + 64) * TROWS, nz), f32),
            pltpu.VMEM(((lines // 2 + 64) * TROWS, nz), f32),
            pltpu.VMEM((steps, lx, ly, nz), f32),
            pltpu.VMEM((steps, lx, ly, nz), f32),
            pltpu.VMEM((lx, ly, nz), f32),
            pltpu.SemaphoreType.DMA((3, lx)),
        ],
        compiler_params=pltpu.CompilerParams(vmem_limit_bytes=48 * 2**20),
        cost_estimate=pl.CostEstimate(flops=10**9, bytes_accessed=80 * 10**6, transcendentals=0),
        name="scatter",
    )(enc, senc, vals, svals)

    levels = 2 * steps + 4
    band = ny // 4
    dma = pltpu.SemaphoreType.DMA
    image = pl.pallas_call(
        wave_kernel,
        out_shape=jax.ShapeDtypeStruct((cx, band, nz), f32),
        in_specs=[anyw] * 11,
        out_specs=vmem,
        scratch_shapes=[
            pltpu.VMEM((levels, lx + 2 * H, ly + 2 * PAD, nz), f32),
            pltpu.VMEM((lx, ly, nz), f32),
            pltpu.VMEM((steps, lx, ly, nz), f32),
            pltpu.VMEM((steps, lx, ly, nz), f32),
            pltpu.VMEM((lx, ly, nz), f32),
            pltpu.VMEM((lx, ly, nz), f32),
            pltpu.VMEM((lx, band, nz), f32),
            pltpu.VMEM((lx, band, nz), f32),
            pltpu.VMEM((2, cx, band, nz), f32),
            dma((levels, 2 * (ly // PIECE) + 1)),
            dma((levels, 2 * (ly // PIECE) + 1)),
            dma((2, cx)),
            dma((2, cx)),
            dma((13,)),
            dma((steps,)),
            dma((3,)),
            dma((3,)),
        ],
        compiler_params=pltpu.CompilerParams(
            collective_id=0, has_side_effects=True, vmem_limit_bytes=60 * 2**20
        ),
        name="waves",
    )(velocity, wave_now, wave_prev, adjoint_now, adjoint_prev, far, same, cross, s_f, o_f, m_f)
    own = lax.dynamic_slice_in_dim(velocity, lax.axis_index("shot") * band, band, 1)
    return -2.0 / (own * own * own) * image


def solution(mesh):
    in_specs = (
        P("space", None, None),
        P("shot", "space", None, None),
        P("shot", "space", None, None),
        P("shot", "space", None, None),
        P("shot", "space", None, None),
        P("shot", None),
        P("shot", None, None),
        P("space"),
        P("space"),
        P("shot", None, "space"),
    )
    out_specs = P("space", "shot", None)
    return jax.shard_map(
        per_device, mesh=mesh, in_specs=in_specs, out_specs=out_specs, check_vma=False
    )
```

```python
import functools

import jax
import jax.numpy as jnp
from jax import lax
from jax.experimental import pallas as pl
from jax.experimental.pallas import tpu as pltpu
from jax.sharding import PartitionSpec as P

TAPS = (-205.0 / 72.0, 8.0 / 5.0, -1.0 / 5.0, 8.0 / 315.0, -1.0 / 560.0)
COURANT = 0.09
MESH = pl.DeviceIdType.MESH
PAD = 8
H = 4
TROWS = 21
CHUNK = 32
PIECE = 32
GROUP = 4


def scatter_kernel(
    enc, senc, vals, svals, s_out, o_out, m_out, low, high, s_v, o_v, m_v, sems
):
    steps, lx, ly, lz = s_v.shape
    half = lx // 2
    slots = enc.shape[1]
    lane = lax.broadcasted_iota(jnp.int32, (8, lz), 1)

    def clear(i, _):
        at = pl.ds(pl.multiple_of(i * 64, 8), 64)
        low[at, :] = jnp.zeros((64, lz), jnp.float32)
        high[at, :] = jnp.zeros((64, lz), jnp.float32)
        return 0

    lax.fori_loop(0, low.shape[0] // 64, clear, 0)

    def place(cells, values, first, tiles):
        def one(j, _):
            places = []
            for h, table in enumerate((low, high)):
                cell = cells[h, first + j]
                line = lax.shift_right_logical(cell, 7)
                z = cell & 127
                shift = (z - j) & 127
                here = lane == z
                for k, tile in enumerate(tiles):
                    value = values[h % values.shape[0], 8 * k : 8 * k + 8, first : first + 128]
                    at = pl.ds(line * TROWS + 8 * tile, 8)
                    added = jnp.where(here, pltpu.roll(value, shift, 1), 0.0)
                    places.append((table, at, table[at, :] + added))
            for table, at, value in places:
                table[at, :] = value
            return 0

        lax.fori_loop(0, 128, one, 0, unroll=8)

    for first in range(0, slots, 128):
        place(enc, vals, first, (0, 1))
    for first in range(0, senc.shape[1], 128):
        place(senc, svals, first, (1, 2))

    def copies(xi):
        return (
            pltpu.make_async_copy(s_v.at[:, xi], s_out.at[:, xi], sems.at[0, xi]),
            pltpu.make_async_copy(o_v.at[:, xi], o_out.at[:, xi], sems.at[1, xi]),
            pltpu.make_async_copy(m_v.at[xi], m_out.at[xi], sems.at[2, xi]),
        )

    for h, table in enumerate((low, high)):

        def spread(x0, _):
            xi = x0 + half * h
            for y0 in range(0, ly, 8):
                base = (x0 * ly + y0) * TROWS
                for t in range(steps):
                    o_v[t, xi, y0 : y0 + 8, :] = table[pl.ds(base + t, 8, stride=TROWS), :]
                    s_v[t, xi, y0 : y0 + 8, :] = table[pl.ds(base + 11 + t, 8, stride=TROWS), :]
                m_v[xi, y0 : y0 + 8, :] = table[pl.ds(base + 10, 8, stride=TROWS), :]
            for copy in copies(xi):
                copy.start()
            return 0

        lax.fori_loop(0, half, spread, 0)

    def finish(xi, _):
        for copy in copies(xi):
            copy.wait()
        return 0

    lax.fori_loop(0, lx, finish, 0)


def wave_kernel(
    vel, now, prev, adj, adjp, far, same, cross, s_hbm, o_hbm, m_hbm, out,
    u, c2, s_v, o_v, m_v, img, pair, red, got,
    halo_send, halo_recv, adj_send, adj_recv, loc, s_sem, red_send, red_recv,
):
    cx, ny, nz = vel.shape
    lx, ly = 2 * cx, ny // 2
    steps = s_hbm.shape[0]
    n_space = lax.axis_size("space")
    i = lax.axis_index("space")
    s = lax.axis_index("shot")
    a, b = i // 2, i % 2
    x, core = s // 2, s % 2
    has_low = a > 0
    has_high = a < n_space // 2 - 1
    other_i = i + 1 - 2 * b
    other_s = s + 1 - 2 * core
    cross_s = s + 2 - 4 * x
    top = 2 * steps + 3

    def zero_low(l, _):
        u[l, 0:H, PAD : PAD + ly, :] = jnp.zeros((H, ly, nz), jnp.float32)
        return 0

    def zero_high(l, _):
        u[l, H + lx : lx + 2 * H, PAD : PAD + ly, :] = jnp.zeros((H, ly, nz), jnp.float32)
        return 0

    def zero_left(l, _):
        u[l, H : H + lx, 0:PAD, :] = jnp.zeros((lx, PAD, nz), jnp.float32)
        return 0

    def zero_right(l, _):
        u[l, H : H + lx, PAD + ly : 2 * PAD + ly, :] = jnp.zeros((lx, PAD, nz), jnp.float32)
        return 0

    @pl.when(jnp.logical_not(has_low))
    def _():
        lax.fori_loop(0, top, zero_low, 0)

    @pl.when(jnp.logical_not(has_high))
    def _():
        lax.fori_loop(0, top, zero_high, 0)

    @pl.when(b == 0)
    def _():
        lax.fori_loop(0, top, zero_left, 0)

    @pl.when(b == 1)
    def _():
        lax.fori_loop(0, top, zero_right, 0)

    level_of = (1, None, 0, steps + 3, steps + 2)
    sources = (now, vel, prev, adj, adjp)
    mine = pl.ds(pl.multiple_of(ly * b, 8), ly)
    theirs = pl.ds(pl.multiple_of(ly * (1 - b), 8), ly)

    def landing(k, half):
        if level_of[k] is None:
            return c2.at[pl.ds(cx * half, cx)]
        return u.at[level_of[k], pl.ds(H + cx * half, cx), PAD : PAD + ly, :]

    def view(k, rows):
        if k == 1:
            return sources[k].at[:, rows, :]
        return sources[k].at[0, :, rows, :]

    def local_copy(k):
        return pltpu.make_async_copy(view(k, mine), landing(k, b), loc.at[k])

    part = pl.ds(cx * (1 - b) + (cx // 2) * core, cx // 2)

    def far_copy(k):
        if k == 1:
            return pltpu.make_async_copy(far.at[2 * cx :], c2.at[part], loc.at[9])
        start = cx * (k // 2)
        return pltpu.make_async_copy(far.at[start : start + cx], landing(k, 1 - b), loc.at[8 + k])

    share = pltpu.make_async_remote_copy(
        src_ref=far.at[2 * cx :], dst_ref=c2.at[part],
        send_sem=red_send.at[4], recv_sem=red_recv.at[4],
        device_id=(i, other_s), device_id_type=MESH,
    )

    def low_copy(first):
        return pltpu.make_async_copy(first, u.at[1, 0:H, PAD : PAD + ly, :], loc.at[11])

    def high_copy(first):
        return pltpu.make_async_copy(
            first, u.at[1, H + lx : lx + 2 * H, PAD : PAD + ly, :], loc.at[12]
        )

    def s_copy(k):
        return pltpu.make_async_copy(s_hbm.at[k], s_v.at[k], s_sem.at[k])

    def partner_layer(k, layer):
        return pltpu.make_async_remote_copy(
            src_ref=sources[k].at[0, layer, theirs, :],
            dst_ref=u.at[level_of[k], H + cx * b + layer, PAD : PAD + ly, :],
            send_sem=adj_send.at[k - 3, layer], recv_sem=adj_recv.at[k - 3, layer],
            device_id=(other_i, s), device_id_type=MESH,
        )

    extra = [
        pltpu.make_async_copy(m_hbm, m_v, loc.at[5]),
        pltpu.make_async_copy(o_hbm, o_v, loc.at[7]),
    ]

    def each_edge(call):
        for parity, low, high in ((0, cross, same), (1, same, cross)):

            @pl.when(jnp.logical_and(b == parity, has_low))
            def _():
                call(low_copy(low))

            @pl.when(jnp.logical_and(b == parity, has_high))
            def _():
                call(high_copy(high))

    for k in range(3):
        local_copy(k).start()
        far_copy(k).start()
    each_edge(lambda copy: copy.start())
    for k in range(steps):
        s_copy(k).start()
    for k in (3, 4):
        local_copy(k).start()
    for copy in extra:
        copy.start()

    barrier = pltpu.get_barrier_semaphore()
    for target in ((other_i, s), (i, other_s), (i, cross_s), (other_i, cross_s)):
        pl.semaphore_signal(barrier, inc=1, device_id=target, device_id_type=MESH)

    @pl.when(has_low)
    def _():
        pl.semaphore_signal(barrier, inc=1, device_id=(i - 2, s), device_id_type=MESH)

    @pl.when(has_high)
    def _():
        pl.semaphore_signal(barrier, inc=1, device_id=(i + 2, s), device_id_type=MESH)

    pl.semaphore_wait(barrier, 4 + has_low.astype(jnp.int32) + has_high.astype(jnp.int32))
    share.start()


    pieces = ly // PIECE

    def send_up(l, p):
        rows = slice(PAD + PIECE * p, PAD + PIECE * (p + 1))
        return pltpu.make_async_remote_copy(
            src_ref=u.at[l, lx : lx + H, rows, :],
            dst_ref=u.at[l, 0:H, rows, :],
            send_sem=halo_send.at[l, p], recv_sem=halo_recv.at[l, p],
            device_id=(i + 2, s), device_id_type=MESH,
        )

    def send_down(l, p):
        rows = slice(PAD + PIECE * p, PAD + PIECE * (p + 1))
        return pltpu.make_async_remote_copy(
            src_ref=u.at[l, H : 2 * H, rows, :],
            dst_ref=u.at[l, lx + H : lx + 2 * H, rows, :],
            send_sem=halo_send.at[l, pieces + p], recv_sem=halo_recv.at[l, pieces + p],
            device_id=(i - 2, s), device_id_type=MESH,
        )

    def send_side(l):
        return pltpu.make_async_remote_copy(
            src_ref=u.at[l, H : H + lx, pl.ds(pl.multiple_of(ly - (ly - PAD) * b, 8), PAD), :],
            dst_ref=u.at[l, H : H + lx, pl.ds(pl.multiple_of((ly + PAD) * b, 8), PAD), :],
            send_sem=halo_send.at[l, 2 * pieces], recv_sem=halo_recv.at[l, 2 * pieces],
            device_id=(other_i, s), device_id_type=MESH,
        )

    def start_down(l, p):
        @pl.when(has_low)
        def _():
            send_down(l, p).start()

    def start_up(l, p):
        @pl.when(has_high)
        def _():
            send_up(l, p).start()

    def start_all(l, order):
        send_side(l).start()
        for p in order:
            start_down(l, p)
            start_up(l, p)

    def wait_low(l, p, arrives):
        @pl.when(jnp.logical_and(has_low, arrives))
        def _():
            send_up(l, p).wait_recv()
            send_down(l, p).wait_send()

    def wait_high(l, p, arrives):
        @pl.when(jnp.logical_and(has_high, arrives))
        def _():
            send_down(l, p).wait_recv()
            send_up(l, p).wait_send()

    def settle(k):
        local_copy(k).wait()
        far_copy(k).wait()

    lane = lax.broadcasted_iota(jnp.int32, (CHUNK, nz), 1)

    def laplace(l, xi, r0):
        rows = lambda d: slice(PAD + r0 + d, PAD + r0 + d + CHUNK)
        centre = u[l, H + xi, rows(0), :]
        result = 3.0 * TAPS[0] * centre
        for k in range(1, H + 1):
            beside = u[l, H + xi + k, rows(0), :] + u[l, H + xi - k, rows(0), :]
            beside = beside + (u[l, H + xi, rows(k), :] + u[l, H + xi, rows(-k), :])
            above = jnp.where(lane < nz - k, pltpu.roll(centre, nz - k, 1), 0.0)
            below = jnp.where(lane >= k, pltpu.roll(centre, k, 1), 0.0)
            result = result + TAPS[k] * (beside + (above + below))
        return centre, result

    def sweep(first, last, p, body):
        def group(g, _):
            writes = []
            for j in range(GROUP):
                writes += body(first + g * GROUP + j, PIECE * p)
            for ref, at, value in writes:
                ref[at] = value
            return 0

        count = (last - first) // GROUP
        if count == 1:
            group(0, 0)
        else:
            lax.fori_loop(0, count, group, 0)

    def step(cur, arrives, more, order, cell):
        for n, p in enumerate(order):
            if n == 0:
                send_side(cur).wait()
            wait_low(cur, p, arrives)
            sweep(0, H, p, cell)

            @pl.when(more)
            def _():
                start_down(cur + 1, p)

            wait_high(cur, p, arrives)
            sweep(lx - H, lx, p, cell)

            @pl.when(more)
            def _():
                start_up(cur + 1, p)

            sweep(H, lx - H, p, cell)
            if n == 0:

                @pl.when(more)
                def _():
                    send_side(cur + 1).start()

    def square(xi, r0):
        value = COURANT * c2[xi, r0 : r0 + CHUNK, :]
        at = (xi, slice(r0, r0 + CHUNK))
        return [(c2, at, value * value), (img, at, jnp.zeros((CHUNK, nz), jnp.float32))]

    def forward(order, t, _):
        cur = t + 1

        def cell(xi, r0):
            rows = slice(PAD + r0, PAD + r0 + CHUNK)
            inner = slice(r0, r0 + CHUNK)
            centre, lap = laplace(cur, xi, r0)
            fresh = 2.0 * centre - u[t, H + xi, rows, :] + c2[xi, inner, :] * lap
            return [(u, (t + 2, H + xi, rows), fresh + s_v[t, xi, inner, :])]

        @pl.when(t < cx)
        def _():
            partner_layer(3, t).start()
            partner_layer(4, t).start()

        s_copy(t).wait()
        step(cur, t > 0, t < steps - 1, order, cell)

        @pl.when(t == steps - 2)
        def _():
            for k in (3, 4):
                local_copy(k).wait()

                def arrive(layer, _):
                    partner_layer(k, layer).wait()
                    return 0

                lax.fori_loop(0, cx, arrive, 0)
            start_all(steps + 3, order)

        return 0

    def backward(order, k, _):
        t = steps - 1 - k
        cur = steps + 3 + k

        def cell(xi, r0):
            rows = slice(PAD + r0, PAD + r0 + CHUNK)
            inner = slice(r0, r0 + CHUNK)
            centre, lap = laplace(cur, xi, r0)
            fresh = 2.0 * centre - u[cur - 1, H + xi, rows, :] + c2[xi, inner, :] * lap
            later = u[t + 2, H + xi, rows, :]
            fresh = fresh + m_v[xi, inner, :] * (later - o_v[t, xi, inner, :])
            accel = later - 2.0 * u[t + 1, H + xi, rows, :] + u[t, H + xi, rows, :]
            total = img[xi, inner, :] + fresh * accel
            return [(img, (xi, inner), total), (u, (cur + 1, H + xi, rows), fresh)]

        step(cur, True, k < steps - 1, order, cell)
        return 0

    def both(order):
        settle(0)
        send_side(1).start()
        settle(1)
        share.wait()
        for p in order:
            sweep(0, lx, p, square)
        settle(2)
        each_edge(lambda copy: copy.wait())
        lax.fori_loop(0, steps, functools.partial(forward, order), 0)
        for copy in extra:
            copy.wait()
        lax.fori_loop(0, steps, functools.partial(backward, order), 0)

    @pl.when(b == 0)
    def _():
        both(tuple(range(pieces - 1, -1, -1)))

    @pl.when(b == 1)
    def _():
        both(tuple(range(pieces)))

    band = out.shape[1]
    keep = pl.multiple_of(band * core, 8)
    give = pl.multiple_of(band * (1 - core), 8)
    def swap(half):
        layers = slice(cx * half, cx * (half + 1))
        return pltpu.make_async_remote_copy(
            src_ref=img.at[layers, pl.ds(give, band), :], dst_ref=pair.at[layers],
            send_sem=red_send.at[2 + half], recv_sem=red_recv.at[2 + half],
            device_id=(i, other_s), device_id_type=MESH,
        )

    for half in range(2):
        swap(half).start()

    def deliver(target):
        return pltpu.make_async_remote_copy(
            src_ref=red.at[pl.ds(cx * target, cx)], dst_ref=got.at[x],
            send_sem=red_send.at[target], recv_sem=red_recv.at[x],
            device_id=(2 * a + target, 2 * b + core), device_id_type=MESH,
        )

    def arrival(k):
        return pltpu.make_async_remote_copy(
            src_ref=red.at[0:cx], dst_ref=got.at[k],
            send_sem=red_send.at[k], recv_sem=red_recv.at[k],
            device_id=(other_i, s), device_id_type=MESH,
        )

    for target in range(2):
        swap(target).wait()
        for xi in range(cx * target, cx * (target + 1)):
            red[xi] = img[xi, pl.ds(keep, band), :] + pair[xi]
        own = jnp.logical_and(x == b, b == target)

        @pl.when(jnp.logical_not(own))
        def _():
            deliver(target).start()

        @pl.when(own)
        def _():
            got[target] = red[cx * target : cx * (target + 1)]

    for k in range(2):
        own = jnp.logical_and(x == b, x == k)

        @pl.when(jnp.logical_not(own))
        def _():
            arrival(k).wait_recv()
            deliver(k).wait_send()

    for xi in range(cx):
        out[xi] = got[0, xi] + got[1, xi]


def per_device(
    velocity, wave_now, wave_prev, adjoint_now, adjoint_prev,
    source_cells, wavelet, receiver_cells, receiver_counts, observed,
):
    cx, ny, nz = velocity.shape
    lx, ly = 2 * cx, ny // 2
    lines = lx * ly
    steps = wavelet.shape[1]
    slots = receiver_cells.shape[0]
    count = lax.axis_size("space")
    i = lax.axis_index("space")
    a, b = i // 2, i % 2
    swap = [(j, j + 1 - 2 * (j % 2)) for j in range(count)]

    live = jnp.arange(slots, dtype=jnp.int32) < receiver_counts[0]
    own_cells = jnp.where(live, receiver_cells, -1)
    their_cells = lax.ppermute(own_cells, "space", swap)
    their_obs = lax.ppermute(observed[0], "space", swap)

    def rows_of(block, part):
        return lax.dynamic_slice_in_dim(block, ly * part, ly, 1)

    core = lax.axis_index("shot") % 2
    part = lax.dynamic_slice_in_dim(velocity, (cx // 2) * core, cx // 2, 0)
    far = jnp.concatenate([rows_of(f, 1 - b) for f in (wave_now[0], wave_prev[0], part)])
    far = lax.ppermute(far, "space", swap)
    edge = lax.dynamic_slice_in_dim(wave_now[0], (cx - H) * b, H, 0)
    beyond = [(j, j + 4 * (j % 2) - 2) for j in range(count)]
    across = [(j, j + 2 * (j % 2) - 1) for j in range(count)]
    within = lambda pairs: [(j, k) for j, k in pairs if 0 <= k < count]
    same = lax.ppermute(rows_of(edge, b), "space", within(beyond))
    cross = lax.ppermute(rows_of(edge, 1 - b), "space", within(across))

    def code(cells, layer0, layers):
        line = cells // nz
        xg = line // ny + layer0
        yl = line % ny - ly * b
        ok = (cells >= 0) & (xg >= 0) & (xg < layers) & (yl >= 0) & (yl < ly)
        return jnp.where(ok, (xg * ly + yl) * nz + cells % nz, lines // 2 * nz)

    first = b == 0
    enc = code(
        jnp.stack([jnp.where(first, own_cells, their_cells), jnp.where(first, their_cells, own_cells)]),
        0, cx,
    )
    senc = jnp.stack([code(source_cells[0], -lx * a - cx * h, cx) for h in range(2)])
    vals = jnp.stack(
        [jnp.where(first, observed[0], their_obs), jnp.where(first, their_obs, observed[0])]
    )
    ones = jnp.ones((2, 1, slots), jnp.float32)
    vals = jnp.concatenate([vals, ones, jnp.zeros((2, 5, slots), jnp.float32)], axis=1)
    w = wavelet[0]
    gap = jnp.zeros((3, w.shape[1]), jnp.float32)
    svals = jnp.concatenate([gap, w, gap], axis=0)[None]

    smem = pl.BlockSpec(memory_space=pltpu.SMEM)
    vmem = pl.BlockSpec(memory_space=pltpu.VMEM)
    anyw = pl.BlockSpec(memory_space=pl.ANY)
    f32 = jnp.float32
    dense = jax.ShapeDtypeStruct((steps, lx, ly, nz), f32)
    field = jax.ShapeDtypeStruct((lx, ly, nz), f32)
    s_f, o_f, m_f = pl.pallas_call(
        scatter_kernel,
        out_shape=(dense, dense, field),
        in_specs=[smem, smem, vmem, vmem],
        out_specs=(anyw, anyw, anyw),
        scratch_shapes=[
            pltpu.VMEM(((lines // 2 + 64) * TROWS, nz), f32),
            pltpu.VMEM(((lines // 2 + 64) * TROWS, nz), f32),
            pltpu.VMEM((steps, lx, ly, nz), f32),
            pltpu.VMEM((steps, lx, ly, nz), f32),
            pltpu.VMEM((lx, ly, nz), f32),
            pltpu.SemaphoreType.DMA((3, lx)),
        ],
        compiler_params=pltpu.CompilerParams(vmem_limit_bytes=48 * 2**20),
        cost_estimate=pl.CostEstimate(flops=10**9, bytes_accessed=80 * 10**6, transcendentals=0),
        name="scatter",
    )(enc, senc, vals, svals)

    levels = 2 * steps + 4
    band = ny // 4
    dma = pltpu.SemaphoreType.DMA
    image = pl.pallas_call(
        wave_kernel,
        out_shape=jax.ShapeDtypeStruct((cx, band, nz), f32),
        in_specs=[anyw] * 11,
        out_specs=vmem,
        scratch_shapes=[
            pltpu.VMEM((levels, lx + 2 * H, ly + 2 * PAD, nz), f32),
            pltpu.VMEM((lx, ly, nz), f32),
            pltpu.VMEM((steps, lx, ly, nz), f32),
            pltpu.VMEM((steps, lx, ly, nz), f32),
            pltpu.VMEM((lx, ly, nz), f32),
            pltpu.VMEM((lx, ly, nz), f32),
            pltpu.VMEM((lx, band, nz), f32),
            pltpu.VMEM((lx, band, nz), f32),
            pltpu.VMEM((2, cx, band, nz), f32),
            dma((levels, 2 * (ly // PIECE) + 1)),
            dma((levels, 2 * (ly // PIECE) + 1)),
            dma((2, cx)),
            dma((2, cx)),
            dma((13,)),
            dma((steps,)),
            dma((5,)),
            dma((5,)),
        ],
        compiler_params=pltpu.CompilerParams(
            collective_id=0, has_side_effects=True, vmem_limit_bytes=60 * 2**20
        ),
        name="waves",
    )(velocity, wave_now, wave_prev, adjoint_now, adjoint_prev, far, same, cross, s_f, o_f, m_f)
    own = lax.dynamic_slice_in_dim(velocity, lax.axis_index("shot") * band, band, 1)
    return -2.0 / (own * own * own) * image


def solution(mesh):
    in_specs = (
        P("space", None, None),
        P("shot", "space", None, None),
        P("shot", "space", None, None),
        P("shot", "space", None, None),
        P("shot", "space", None, None),
        P("shot", None),
        P("shot", None, None),
        P("space"),
        P("space"),
        P("shot", None, "space"),
    )
    out_specs = P("space", "shot", None)
    return jax.shard_map(
        per_device, mesh=mesh, in_specs=in_specs, out_specs=out_specs, check_vma=False
    )
```

```python
import functools

import jax
import jax.numpy as jnp
from jax import lax
from jax.experimental import pallas as pl
from jax.experimental.pallas import tpu as pltpu
from jax.sharding import PartitionSpec as P

TAPS = (-205.0 / 72.0, 8.0 / 5.0, -1.0 / 5.0, 8.0 / 315.0, -1.0 / 560.0)
COURANT = 0.09
MESH = pl.DeviceIdType.MESH
PAD = 8
H = 4
TROWS = 21
CHUNK = 32
PIECE = 32
GROUP = 4


def scatter_kernel(
    enc, senc, vals, svals, s_out, o_out, m_out, low, high, s_v, o_v, m_v, sems
):
    steps, lx, ly, lz = s_v.shape
    half = lx // 2
    slots = enc.shape[1]
    lane = lax.broadcasted_iota(jnp.int32, (8, lz), 1)

    def clear(i, _):
        at = pl.ds(pl.multiple_of(i * 64, 8), 64)
        low[at, :] = jnp.zeros((64, lz), jnp.float32)
        high[at, :] = jnp.zeros((64, lz), jnp.float32)
        return 0

    lax.fori_loop(0, low.shape[0] // 64, clear, 0)

    def place(cells, values, first, tiles, batch):
        def one(i, _):
            places = []
            for h, table in enumerate((low, high)):
                before = []
                for n in range(batch):
                    j = i * batch + n
                    cell = cells[h, first + j]
                    line = lax.shift_right_logical(cell, 7)
                    z = cell & 127
                    shift = (z - j) & 127
                    here = lane == z
                    terms = []
                    for k, tile in enumerate(tiles):
                        value = values[h % values.shape[0], 8 * k : 8 * k + 8, first : first + 128]
                        at = pl.ds(line * TROWS + 8 * tile, 8)
                        term = jnp.where(here, pltpu.roll(value, shift, 1), 0.0)
                        terms.append(term)
                        total = table[at, :] + term
                        for other, others in before:
                            total = total + jnp.where(other == line, others[k], 0.0)
                        places.append((table, at, total))
                    before.append((line, terms))
            for table, at, value in places:
                table[at, :] = value
            return 0

        lax.fori_loop(0, 128 // batch, one, 0, unroll=max(1, 8 // batch))

    for first in range(0, slots, 128):
        place(enc, vals, first, (0, 1), 4)
    for first in range(0, senc.shape[1], 128):
        place(senc, svals, first, (1, 2), 1)

    def copies(xi):
        return (
            pltpu.make_async_copy(s_v.at[:, xi], s_out.at[:, xi], sems.at[0, xi]),
            pltpu.make_async_copy(o_v.at[:, xi], o_out.at[:, xi], sems.at[1, xi]),
            pltpu.make_async_copy(m_v.at[xi], m_out.at[xi], sems.at[2, xi]),
        )

    for h, table in enumerate((low, high)):

        def spread(x0, _):
            xi = x0 + half * h
            for y0 in range(0, ly, 8):
                base = (x0 * ly + y0) * TROWS
                for t in range(steps):
                    o_v[t, xi, y0 : y0 + 8, :] = table[pl.ds(base + t, 8, stride=TROWS), :]
                    s_v[t, xi, y0 : y0 + 8, :] = table[pl.ds(base + 11 + t, 8, stride=TROWS), :]
                m_v[xi, y0 : y0 + 8, :] = table[pl.ds(base + 10, 8, stride=TROWS), :]
            for copy in copies(xi):
                copy.start()
            return 0

        lax.fori_loop(0, half, spread, 0)

    def finish(xi, _):
        for copy in copies(xi):
            copy.wait()
        return 0

    lax.fori_loop(0, lx, finish, 0)


def wave_kernel(
    vel, now, prev, adj, adjp, far, same, cross, s_hbm, o_hbm, m_hbm, out,
    u, c2, s_v, o_v, m_v, img, pair, red, got,
    halo_send, halo_recv, adj_send, adj_recv, loc, s_sem, red_send, red_recv,
):
    cx, ny, nz = vel.shape
    lx, ly = 2 * cx, ny // 2
    steps = s_hbm.shape[0]
    n_space = lax.axis_size("space")
    i = lax.axis_index("space")
    s = lax.axis_index("shot")
    a, b = i // 2, i % 2
    x, core = s // 2, s % 2
    has_low = a > 0
    has_high = a < n_space // 2 - 1
    other_i = i + 1 - 2 * b
    other_s = s + 1 - 2 * core
    cross_s = s + 2 - 4 * x
    top = 2 * steps + 3

    def zero_low(l, _):
        u[l, 0:H, PAD : PAD + ly, :] = jnp.zeros((H, ly, nz), jnp.float32)
        return 0

    def zero_high(l, _):
        u[l, H + lx : lx + 2 * H, PAD : PAD + ly, :] = jnp.zeros((H, ly, nz), jnp.float32)
        return 0

    def zero_left(l, _):
        u[l, H : H + lx, 0:PAD, :] = jnp.zeros((lx, PAD, nz), jnp.float32)
        return 0

    def zero_right(l, _):
        u[l, H : H + lx, PAD + ly : 2 * PAD + ly, :] = jnp.zeros((lx, PAD, nz), jnp.float32)
        return 0

    @pl.when(jnp.logical_not(has_low))
    def _():
        lax.fori_loop(0, top, zero_low, 0)

    @pl.when(jnp.logical_not(has_high))
    def _():
        lax.fori_loop(0, top, zero_high, 0)

    @pl.when(b == 0)
    def _():
        lax.fori_loop(0, top, zero_left, 0)

    @pl.when(b == 1)
    def _():
        lax.fori_loop(0, top, zero_right, 0)

    level_of = (1, None, 0, steps + 3, steps + 2)
    sources = (now, vel, prev, adj, adjp)
    mine = pl.ds(pl.multiple_of(ly * b, 8), ly)
    theirs = pl.ds(pl.multiple_of(ly * (1 - b), 8), ly)

    def landing(k, half):
        if level_of[k] is None:
            return c2.at[pl.ds(cx * half, cx)]
        return u.at[level_of[k], pl.ds(H + cx * half, cx), PAD : PAD + ly, :]

    def view(k, rows):
        if k == 1:
            return sources[k].at[:, rows, :]
        return sources[k].at[0, :, rows, :]

    def local_copy(k):
        return pltpu.make_async_copy(view(k, mine), landing(k, b), loc.at[k])

    part = pl.ds(cx * (1 - b) + (cx // 2) * core, cx // 2)

    def far_copy(k):
        if k == 1:
            return pltpu.make_async_copy(far.at[2 * cx :], c2.at[part], loc.at[9])
        start = cx * (k // 2)
        return pltpu.make_async_copy(far.at[start : start + cx], landing(k, 1 - b), loc.at[8 + k])

    share = pltpu.make_async_remote_copy(
        src_ref=far.at[2 * cx :], dst_ref=c2.at[part],
        send_sem=red_send.at[4], recv_sem=red_recv.at[4],
        device_id=(i, other_s), device_id_type=MESH,
    )

    def low_copy(first):
        return pltpu.make_async_copy(first, u.at[1, 0:H, PAD : PAD + ly, :], loc.at[11])

    def high_copy(first):
        return pltpu.make_async_copy(
            first, u.at[1, H + lx : lx + 2 * H, PAD : PAD + ly, :], loc.at[12]
        )

    def s_copy(k):
        return pltpu.make_async_copy(s_hbm.at[k], s_v.at[k], s_sem.at[k])

    def partner_layer(k, layer):
        return pltpu.make_async_remote_copy(
            src_ref=sources[k].at[0, layer, theirs, :],
            dst_ref=u.at[level_of[k], H + cx * b + layer, PAD : PAD + ly, :],
            send_sem=adj_send.at[k - 3, layer], recv_sem=adj_recv.at[k - 3, layer],
            device_id=(other_i, s), device_id_type=MESH,
        )

    extra = [
        pltpu.make_async_copy(m_hbm, m_v, loc.at[5]),
        pltpu.make_async_copy(o_hbm, o_v, loc.at[7]),
    ]

    def each_edge(call):
        for parity, low, high in ((0, cross, same), (1, same, cross)):

            @pl.when(jnp.logical_and(b == parity, has_low))
            def _():
                call(low_copy(low))

            @pl.when(jnp.logical_and(b == parity, has_high))
            def _():
                call(high_copy(high))

    for k in range(3):
        local_copy(k).start()
        far_copy(k).start()
    each_edge(lambda copy: copy.start())
    for k in range(steps):
        s_copy(k).start()
    for k in (3, 4):
        local_copy(k).start()
    for copy in extra:
        copy.start()

    barrier = pltpu.get_barrier_semaphore()
    for target in ((other_i, s), (i, other_s), (i, cross_s), (other_i, cross_s)):
        pl.semaphore_signal(barrier, inc=1, device_id=target, device_id_type=MESH)

    @pl.when(has_low)
    def _():
        pl.semaphore_signal(barrier, inc=1, device_id=(i - 2, s), device_id_type=MESH)

    @pl.when(has_high)
    def _():
        pl.semaphore_signal(barrier, inc=1, device_id=(i + 2, s), device_id_type=MESH)

    pl.semaphore_wait(barrier, 4 + has_low.astype(jnp.int32) + has_high.astype(jnp.int32))
    share.start()


    pieces = ly // PIECE

    def send_up(l, p):
        rows = slice(PAD + PIECE * p, PAD + PIECE * (p + 1))
        return pltpu.make_async_remote_copy(
            src_ref=u.at[l, lx : lx + H, rows, :],
            dst_ref=u.at[l, 0:H, rows, :],
            send_sem=halo_send.at[l, p], recv_sem=halo_recv.at[l, p],
            device_id=(i + 2, s), device_id_type=MESH,
        )

    def send_down(l, p):
        rows = slice(PAD + PIECE * p, PAD + PIECE * (p + 1))
        return pltpu.make_async_remote_copy(
            src_ref=u.at[l, H : 2 * H, rows, :],
            dst_ref=u.at[l, lx + H : lx + 2 * H, rows, :],
            send_sem=halo_send.at[l, pieces + p], recv_sem=halo_recv.at[l, pieces + p],
            device_id=(i - 2, s), device_id_type=MESH,
        )

    def send_side(l):
        return pltpu.make_async_remote_copy(
            src_ref=u.at[l, H : H + lx, pl.ds(pl.multiple_of(ly - (ly - PAD) * b, 8), PAD), :],
            dst_ref=u.at[l, H : H + lx, pl.ds(pl.multiple_of((ly + PAD) * b, 8), PAD), :],
            send_sem=halo_send.at[l, 2 * pieces], recv_sem=halo_recv.at[l, 2 * pieces],
            device_id=(other_i, s), device_id_type=MESH,
        )

    def start_down(l, p):
        @pl.when(has_low)
        def _():
            send_down(l, p).start()

    def start_up(l, p):
        @pl.when(has_high)
        def _():
            send_up(l, p).start()

    def start_all(l, order):
        send_side(l).start()
        for p in order:
            start_down(l, p)
            start_up(l, p)

    def wait_low(l, p, arrives):
        @pl.when(jnp.logical_and(has_low, arrives))
        def _():
            send_up(l, p).wait_recv()
            send_down(l, p).wait_send()

    def wait_high(l, p, arrives):
        @pl.when(jnp.logical_and(has_high, arrives))
        def _():
            send_down(l, p).wait_recv()
            send_up(l, p).wait_send()

    def settle(k):
        local_copy(k).wait()
        far_copy(k).wait()

    lane = lax.broadcasted_iota(jnp.int32, (CHUNK, nz), 1)

    def laplace(l, xi, r0):
        rows = lambda d: slice(PAD + r0 + d, PAD + r0 + d + CHUNK)
        centre = u[l, H + xi, rows(0), :]
        result = 3.0 * TAPS[0] * centre
        for k in range(1, H + 1):
            beside = u[l, H + xi + k, rows(0), :] + u[l, H + xi - k, rows(0), :]
            beside = beside + (u[l, H + xi, rows(k), :] + u[l, H + xi, rows(-k), :])
            above = jnp.where(lane < nz - k, pltpu.roll(centre, nz - k, 1), 0.0)
            below = jnp.where(lane >= k, pltpu.roll(centre, k, 1), 0.0)
            result = result + TAPS[k] * (beside + (above + below))
        return centre, result

    def sweep(first, last, p, body):
        def group(g, _):
            writes = []
            for j in range(GROUP):
                writes += body(first + g * GROUP + j, PIECE * p)
            for ref, at, value in writes:
                ref[at] = value
            return 0

        count = (last - first) // GROUP
        if count == 1:
            group(0, 0)
        else:
            lax.fori_loop(0, count, group, 0)

    def step(cur, arrives, more, order, cell):
        for n, p in enumerate(order):
            if n == 0:
                send_side(cur).wait()
            wait_low(cur, p, arrives)
            sweep(0, H, p, cell)

            @pl.when(more)
            def _():
                start_down(cur + 1, p)

            wait_high(cur, p, arrives)
            sweep(lx - H, lx, p, cell)

            @pl.when(more)
            def _():
                start_up(cur + 1, p)

            sweep(H, lx - H, p, cell)
            if n == 0:

                @pl.when(more)
                def _():
                    send_side(cur + 1).start()

    def square(xi, r0):
        value = COURANT * c2[xi, r0 : r0 + CHUNK, :]
        at = (xi, slice(r0, r0 + CHUNK))
        return [(c2, at, value * value), (img, at, jnp.zeros((CHUNK, nz), jnp.float32))]

    def forward(order, t, _):
        cur = t + 1

        def cell(xi, r0):
            rows = slice(PAD + r0, PAD + r0 + CHUNK)
            inner = slice(r0, r0 + CHUNK)
            centre, lap = laplace(cur, xi, r0)
            fresh = 2.0 * centre - u[t, H + xi, rows, :] + c2[xi, inner, :] * lap
            return [(u, (t + 2, H + xi, rows), fresh + s_v[t, xi, inner, :])]

        @pl.when(t < cx)
        def _():
            partner_layer(3, t).start()
            partner_layer(4, t).start()

        s_copy(t).wait()
        step(cur, t > 0, t < steps - 1, order, cell)

        @pl.when(t == steps - 2)
        def _():
            for k in (3, 4):
                local_copy(k).wait()

                def arrive(layer, _):
                    partner_layer(k, layer).wait()
                    return 0

                lax.fori_loop(0, cx, arrive, 0)
            start_all(steps + 3, order)

        return 0

    def backward(order, k, _):
        t = steps - 1 - k
        cur = steps + 3 + k

        def cell(xi, r0):
            rows = slice(PAD + r0, PAD + r0 + CHUNK)
            inner = slice(r0, r0 + CHUNK)
            centre, lap = laplace(cur, xi, r0)
            fresh = 2.0 * centre - u[cur - 1, H + xi, rows, :] + c2[xi, inner, :] * lap
            later = u[t + 2, H + xi, rows, :]
            fresh = fresh + m_v[xi, inner, :] * (later - o_v[t, xi, inner, :])
            accel = later - 2.0 * u[t + 1, H + xi, rows, :] + u[t, H + xi, rows, :]
            total = img[xi, inner, :] + fresh * accel
            return [(img, (xi, inner), total), (u, (cur + 1, H + xi, rows), fresh)]

        step(cur, True, k < steps - 1, order, cell)
        return 0

    def both(order):
        settle(0)
        send_side(1).start()
        settle(1)
        share.wait()
        for p in order:
            sweep(0, lx, p, square)
        settle(2)
        each_edge(lambda copy: copy.wait())
        lax.fori_loop(0, steps, functools.partial(forward, order), 0)
        for copy in extra:
            copy.wait()
        lax.fori_loop(0, steps, functools.partial(backward, order), 0)

    @pl.when(b == 0)
    def _():
        both(tuple(range(pieces - 1, -1, -1)))

    @pl.when(b == 1)
    def _():
        both(tuple(range(pieces)))

    band = out.shape[1]
    keep = pl.multiple_of(band * core, 8)
    give = pl.multiple_of(band * (1 - core), 8)
    def swap(half):
        layers = slice(cx * half, cx * (half + 1))
        return pltpu.make_async_remote_copy(
            src_ref=img.at[layers, pl.ds(give, band), :], dst_ref=pair.at[layers],
            send_sem=red_send.at[2 + half], recv_sem=red_recv.at[2 + half],
            device_id=(i, other_s), device_id_type=MESH,
        )

    for half in range(2):
        swap(half).start()

    def deliver(target):
        return pltpu.make_async_remote_copy(
            src_ref=red.at[pl.ds(cx * target, cx)], dst_ref=got.at[x],
            send_sem=red_send.at[target], recv_sem=red_recv.at[x],
            device_id=(2 * a + target, 2 * b + core), device_id_type=MESH,
        )

    def arrival(k):
        return pltpu.make_async_remote_copy(
            src_ref=red.at[0:cx], dst_ref=got.at[k],
            send_sem=red_send.at[k], recv_sem=red_recv.at[k],
            device_id=(other_i, s), device_id_type=MESH,
        )

    for target in range(2):
        swap(target).wait()
        for xi in range(cx * target, cx * (target + 1)):
            red[xi] = img[xi, pl.ds(keep, band), :] + pair[xi]
        own = jnp.logical_and(x == b, b == target)

        @pl.when(jnp.logical_not(own))
        def _():
            deliver(target).start()

        @pl.when(own)
        def _():
            got[target] = red[cx * target : cx * (target + 1)]

    for k in range(2):
        own = jnp.logical_and(x == b, x == k)

        @pl.when(jnp.logical_not(own))
        def _():
            arrival(k).wait_recv()
            deliver(k).wait_send()

    for xi in range(cx):
        out[xi] = got[0, xi] + got[1, xi]


def per_device(
    velocity, wave_now, wave_prev, adjoint_now, adjoint_prev,
    source_cells, wavelet, receiver_cells, receiver_counts, observed,
):
    cx, ny, nz = velocity.shape
    lx, ly = 2 * cx, ny // 2
    lines = lx * ly
    steps = wavelet.shape[1]
    slots = receiver_cells.shape[0]
    count = lax.axis_size("space")
    i = lax.axis_index("space")
    a, b = i // 2, i % 2
    swap = [(j, j + 1 - 2 * (j % 2)) for j in range(count)]

    live = jnp.arange(slots, dtype=jnp.int32) < receiver_counts[0]
    own_cells = jnp.where(live, receiver_cells, -1)
    their_cells = lax.ppermute(own_cells, "space", swap)
    their_obs = lax.ppermute(observed[0], "space", swap)

    def rows_of(block, part):
        return lax.dynamic_slice_in_dim(block, ly * part, ly, 1)

    core = lax.axis_index("shot") % 2
    part = lax.dynamic_slice_in_dim(velocity, (cx // 2) * core, cx // 2, 0)
    far = jnp.concatenate([rows_of(f, 1 - b) for f in (wave_now[0], wave_prev[0], part)])
    far = lax.ppermute(far, "space", swap)
    edge = lax.dynamic_slice_in_dim(wave_now[0], (cx - H) * b, H, 0)
    beyond = [(j, j + 4 * (j % 2) - 2) for j in range(count)]
    across = [(j, j + 2 * (j % 2) - 1) for j in range(count)]
    within = lambda pairs: [(j, k) for j, k in pairs if 0 <= k < count]
    same = lax.ppermute(rows_of(edge, b), "space", within(beyond))
    cross = lax.ppermute(rows_of(edge, 1 - b), "space", within(across))

    def code(cells, layer0, layers):
        line = cells // nz
        xg = line // ny + layer0
        yl = line % ny - ly * b
        ok = (cells >= 0) & (xg >= 0) & (xg < layers) & (yl >= 0) & (yl < ly)
        return jnp.where(ok, (xg * ly + yl) * nz + cells % nz, lines // 2 * nz)

    first = b == 0
    enc = code(
        jnp.stack([jnp.where(first, own_cells, their_cells), jnp.where(first, their_cells, own_cells)]),
        0, cx,
    )
    senc = jnp.stack([code(source_cells[0], -lx * a - cx * h, cx) for h in range(2)])
    vals = jnp.stack(
        [jnp.where(first, observed[0], their_obs), jnp.where(first, their_obs, observed[0])]
    )
    ones = jnp.ones((2, 1, slots), jnp.float32)
    vals = jnp.concatenate([vals, ones, jnp.zeros((2, 5, slots), jnp.float32)], axis=1)
    w = wavelet[0]
    gap = jnp.zeros((3, w.shape[1]), jnp.float32)
    svals = jnp.concatenate([gap, w, gap], axis=0)[None]

    smem = pl.BlockSpec(memory_space=pltpu.SMEM)
    vmem = pl.BlockSpec(memory_space=pltpu.VMEM)
    anyw = pl.BlockSpec(memory_space=pl.ANY)
    f32 = jnp.float32
    dense = jax.ShapeDtypeStruct((steps, lx, ly, nz), f32)
    field = jax.ShapeDtypeStruct((lx, ly, nz), f32)
    s_f, o_f, m_f = pl.pallas_call(
        scatter_kernel,
        out_shape=(dense, dense, field),
        in_specs=[smem, smem, vmem, vmem],
        out_specs=(anyw, anyw, anyw),
        scratch_shapes=[
            pltpu.VMEM(((lines // 2 + 64) * TROWS, nz), f32),
            pltpu.VMEM(((lines // 2 + 64) * TROWS, nz), f32),
            pltpu.VMEM((steps, lx, ly, nz), f32),
            pltpu.VMEM((steps, lx, ly, nz), f32),
            pltpu.VMEM((lx, ly, nz), f32),
            pltpu.SemaphoreType.DMA((3, lx)),
        ],
        compiler_params=pltpu.CompilerParams(vmem_limit_bytes=48 * 2**20),
        cost_estimate=pl.CostEstimate(flops=10**9, bytes_accessed=80 * 10**6, transcendentals=0),
        name="scatter",
    )(enc, senc, vals, svals)

    levels = 2 * steps + 4
    band = ny // 4
    dma = pltpu.SemaphoreType.DMA
    image = pl.pallas_call(
        wave_kernel,
        out_shape=jax.ShapeDtypeStruct((cx, band, nz), f32),
        in_specs=[anyw] * 11,
        out_specs=vmem,
        scratch_shapes=[
            pltpu.VMEM((levels, lx + 2 * H, ly + 2 * PAD, nz), f32),
            pltpu.VMEM((lx, ly, nz), f32),
            pltpu.VMEM((steps, lx, ly, nz), f32),
            pltpu.VMEM((steps, lx, ly, nz), f32),
            pltpu.VMEM((lx, ly, nz), f32),
            pltpu.VMEM((lx, ly, nz), f32),
            pltpu.VMEM((lx, band, nz), f32),
            pltpu.VMEM((lx, band, nz), f32),
            pltpu.VMEM((2, cx, band, nz), f32),
            dma((levels, 2 * (ly // PIECE) + 1)),
            dma((levels, 2 * (ly // PIECE) + 1)),
            dma((2, cx)),
            dma((2, cx)),
            dma((13,)),
            dma((steps,)),
            dma((5,)),
            dma((5,)),
        ],
        compiler_params=pltpu.CompilerParams(
            collective_id=0, has_side_effects=True, vmem_limit_bytes=60 * 2**20
        ),
        name="waves",
    )(velocity, wave_now, wave_prev, adjoint_now, adjoint_prev, far, same, cross, s_f, o_f, m_f)
    own = lax.dynamic_slice_in_dim(velocity, lax.axis_index("shot") * band, band, 1)
    return -2.0 / (own * own * own) * image


def solution(mesh):
    in_specs = (
        P("space", None, None),
        P("shot", "space", None, None),
        P("shot", "space", None, None),
        P("shot", "space", None, None),
        P("shot", "space", None, None),
        P("shot", None),
        P("shot", None, None),
        P("space"),
        P("space"),
        P("shot", None, "space"),
    )
    out_specs = P("space", "shot", None)
    return jax.shard_map(
        per_device, mesh=mesh, in_specs=in_specs, out_specs=out_specs, check_vma=False
    )
```
